128 devices in a mesh: dp: 4 (over x), ctx: 4 (over y_hi, core), tp: 8 (over z, y_lo).
Axes of the slice: x: 4, y: 4 (y_hi: 2, y_lo: 2; y = y_hi * 2 + y_lo), z: 4, core: 2. Of those that a mesh axis runs over, the one named last changes fastest.
Arguments:
- inputs: bfloat16 [6144, 1024], P(('dp', 'ctx')), may hold values from -6 to 6
- cotangent: bfloat16 [6144, 1024], P(('dp', 'ctx')), may hold values from -6 to 6
- routes: int32 [6144, 8], P(('dp', 'ctx')), may hold values from 0 to 31, all different within a row
- seq_lengths: int32 [4, 3], P('dp'), may hold values from 1 to 1024, as said below
- block_order: int32 [4, 24], P('dp'), may hold values from 0 to 23, as said below
- attn_gain: bfloat16 [1024], P('dp'), may hold values from 0.25 to 1.75
- query_weight: bfloat16 [1024, 1024], P('dp', 'tp'), may hold values from -0.1875 to 0.1875
- key_weight: bfloat16 [1024, 512], P('dp', 'tp'), may hold values from -0.1875 to 0.1875
- value_weight: bfloat16 [1024, 512], P('dp', 'tp'), may hold values from -0.1875 to 0.1875
- output_weight: bfloat16 [1024, 1024], P('dp', 'tp'), may hold values from -0.75 to 0.75
- ffn_gain: bfloat16 [1024], P('dp'), may hold values from 0.25 to 1.75
- router_weight: bfloat16 [1024, 32], P('dp'), may hold values from -0.09375 to 0.09375
- gate_weight: bfloat16 [32, 512, 1024], P(None, 'tp', 'dp'), may hold values from -0.1875 to 0.1875
- up_weight: bfloat16 [32, 512, 1024], P(None, 'tp', 'dp'), may hold values from -0.1875 to 0.1875
- down_weight: bfloat16 [32, 512, 1024], P(None, 'tp', 'dp'), may hold values from -1.5 to 1.5
Outputs:
- block_output: bfloat16 [6144, 1024], P(('dp', 'ctx'))
- input_grad: float32 [6144, 1024], P(('dp', 'ctx'))
- grad_attn_gain: float32 [1024], P('dp')
- grad_query: float32 [1024, 1024], P('dp', 'tp')
- grad_key: float32 [1024, 512], P('dp', 'tp')
- grad_value: float32 [1024, 512], P('dp', 'tp')
- grad_output: float32 [1024, 1024], P('dp', 'tp')
- grad_ffn_gain: float32 [1024], P('dp')
- grad_router: float32 [1024, 32], P('dp')
- grad_gate: float32 [32, 512, 1024], P(None, 'tp', 'dp')
- grad_up: float32 [32, 512, 1024], P(None, 'tp', 'dp')
- grad_down: float32 [32, 512, 1024], P(None, 'tp', 'dp')
The draws below stay inside these ranges and needn't reach their ends.
Inputs may be any that keep to these rules, and one draw needn't show every extreme that they name: `seq_lengths`: each row sums to 1536, and one of its 3 lengths is exactly 1024. `block_order`: each row names every block of its group's stream once; slot j of each ctx index holds a block from j * 4 to (j + 1) * 4 - 1. `routes`: the 8 experts of a row are different.
All inputs are finite; a program needn't handle non-finite values.
Results may differ from the reference program's by a relative error of at most 0.03.
Values may be sent and summed in bfloat16 or wider, within the bound.
No kernel may reach another device: no remote copies, remote signals or barrier semaphores. Data moves between devices by JAX's collectives and lax.ppermute only.
A program may use at most 128 MiB of HBM per device.

```python
import jax
import jax.numpy as jnp
from jax import lax

D = 1024
HEADS = 16
KV_HEADS = 8
HEAD_DIM = 64
EXPERTS = 32
FF = 512
TOPK = 8
BLOCK = 64
BLK_DEV = 6
GROUP = 1536
SEQ_MOST = 1024
TOKENS = 6144
N_DP = 4
N_CTX = 4


def draw_seq_lengths(key, part):
    key = jax.random.fold_in(key, 11)
    keys = jax.random.split(key, 2)
    rest = GROUP - SEQ_MOST
    cuts = jax.random.randint(keys[0], (N_DP,), 1, rest, dtype=jnp.int32)
    shifts = jax.random.randint(keys[1], (N_DP,), 0, 3, dtype=jnp.int32)
    table = jnp.stack([jnp.full((N_DP,), SEQ_MOST, jnp.int32), cuts, rest - cuts], axis=1)
    return jax.vmap(lambda row, shift: jnp.roll(row, shift))(table, shifts).astype(jnp.int32)


def draw_block_order(key, part):
    key = jax.random.fold_in(key, 23)
    keys = jax.random.split(key, N_DP * BLK_DEV)
    perms = jax.vmap(lambda sub: jax.random.permutation(sub, N_CTX))(keys).reshape(N_DP, BLK_DEV, N_CTX)
    rounds = jnp.arange(BLK_DEV, dtype=jnp.int32)[None, :, None] * N_CTX
    blocks = rounds + perms.astype(jnp.int32)
    return jnp.transpose(blocks, (0, 2, 1)).reshape(N_DP, N_CTX * BLK_DEV).astype(jnp.int32)


def block_levels(stream_key, extent, cuts, least, high):
    level = 1.0
    for position, shards_of in cuts:
        draws = jax.random.uniform(jax.random.fold_in(jax.random.fold_in(stream_key, 6), position), (shards_of,), jnp.float32, least / len(cuts), high / len(cuts))
        level = level * jnp.repeat(jnp.exp(draws), extent[position] // shards_of).reshape((-1,) + (1,) * (len(extent) - 1 - position))
    return level


def picks_of(stream_key, rows, number_of, top, lift):
    sequence = jax.random.permutation(jax.random.fold_in(stream_key, 1), number_of)
    boost = sequence
    for power in range(3):
        boost = boost * boost // number_of
    boost = boost * lift // number_of
    chance = jax.random.randint(jax.random.fold_in(stream_key, 2), (rows, number_of), 0, 4096) + boost
    holders = jax.random.permutation(jax.random.fold_in(stream_key, 3), rows)[jnp.arange(number_of) % rows]
    chance = jnp.where(jnp.arange(rows)[:, None] == holders[None, :], 1 << 14, chance)
    priority = chance * number_of + jnp.arange(number_of)
    return lax.top_k(priority.astype(jnp.int32), top)[1].astype(jnp.int32)


def centred(own_key, extent, spread, limit, cuts=(), held_as=jnp.bfloat16):
    values = spread * jax.random.normal(own_key, extent, jnp.float32)
    if cuts:
        values = values * block_levels(own_key, extent, cuts, -0.22, 0.18)
    return jnp.clip(values, -limit, limit).astype(held_as)


def setup_inputs(seed: int = 0) -> dict:
    splits = jax.random.split(jax.random.key(seed), 16)
    inputs = centred(splits[0], (TOKENS, D), 1.0, 6.0, ((0, 16),))
    cotangent = centred(splits[1], (TOKENS, D), 1.0, 6.0, ((0, 16),))
    routes = picks_of(splits[2], TOKENS, EXPERTS, TOPK, 2048)
    seq_lengths = draw_seq_lengths(jax.random.fold_in(splits[15], 71), 0)
    block_order = draw_block_order(jax.random.fold_in(splits[15], 71), 0)
    attn_gain = jnp.clip(1.0 + 0.15 * jax.random.normal(splits[5], (D,), jnp.float32), 0.25, 1.75).astype(jnp.bfloat16)
    query_weight = centred(splits[6], (D, HEADS * HEAD_DIM), D ** -0.5, 0.1875, ((0, 4), (1, 8)))
    key_weight = centred(splits[7], (D, KV_HEADS * HEAD_DIM), D ** -0.5, 0.1875, ((0, 4), (1, 8)))
    value_weight = centred(splits[8], (D, KV_HEADS * HEAD_DIM), D ** -0.5, 0.1875, ((0, 4), (1, 8)))
    output_weight = centred(splits[9], (D, HEADS * HEAD_DIM), HEAD_DIM ** -0.5, 0.75, ((0, 4), (1, 8)))
    ffn_gain = jnp.clip(1.0 + 0.15 * jax.random.normal(splits[10], (D,), jnp.float32), 0.25, 1.75).astype(jnp.bfloat16)
    router_weight = centred(splits[11], (D, EXPERTS), (4 * D) ** -0.5, 0.09375, ((0, 4),))
    gate_weight = centred(splits[12], (EXPERTS, FF, D), D ** -0.5, 0.1875, ((1, 8), (2, 4)))
    up_weight = centred(splits[13], (EXPERTS, FF, D), D ** -0.5, 0.1875, ((1, 8), (2, 4)))
    down_weight = centred(splits[14], (EXPERTS, FF, D), (max(FF // 32, 1)) ** -0.5, 1.5, ((1, 8), (2, 4)))
    return dict(inputs=inputs, cotangent=cotangent, routes=routes, seq_lengths=seq_lengths, block_order=block_order, attn_gain=attn_gain, query_weight=query_weight, key_weight=key_weight, value_weight=value_weight, output_weight=output_weight, ffn_gain=ffn_gain, router_weight=router_weight, gate_weight=gate_weight, up_weight=up_weight, down_weight=down_weight)


EPSILON = 1e-05
NEGATIVE = -1e+30

@jax.custom_vjp
def low(v):
    return lax.optimization_barrier(v.astype(jnp.bfloat16)).astype(jnp.float32)

@jax.custom_vjp
def low_back(v):
    return v

def low_keep(v):
    return (low(v), None)

def low_pass(kept, grad):
    return (grad,)

def back_keep(v):
    return (v, None)

def back_low(kept, grad):
    return (low(grad),)
low.defvjp(low_keep, low_pass)
low_back.defvjp(back_keep, back_low)

def matmul(left, right):
    return jnp.dot(left, right, precision=lax.Precision.HIGHEST, preferred_element_type=jnp.float32)

def rms_norm(values, gain):
    factor = lax.rsqrt(lax.optimization_barrier(jnp.mean(values * values, axis=-1, keepdims=True)) + EPSILON)
    return values * factor * gain

def rotate(values, cosine, sine):
    half = values.shape[-1] // 2
    first = values[..., :half]
    second = values[..., half:]
    return jnp.concatenate([first * cosine - second * sine, second * cosine + first * sine], axis=-1)

def stream_places(order_row, length_row):
    offsets = jnp.arange(BLOCK, dtype=jnp.int32)
    places = (order_row[:, None] * BLOCK + offsets[None, :]).reshape(-1).astype(jnp.int32)
    ends = jnp.cumsum(length_row).astype(jnp.int32)
    passed = (places[:, None] >= ends[None, :]).astype(jnp.int32)
    docs = lax.optimization_barrier(jnp.sum(passed, axis=1)).astype(jnp.int32)
    starts = lax.optimization_barrier(jnp.sum(passed * length_row[None, :], axis=1)).astype(jnp.int32)
    return (places, docs, (places - starts).astype(jnp.int32))

def group_forward(weights, rows, places, docs, inner, route_rows):
    attn_gain, query_weight, key_weight, value_weight, output_weight, ffn_gain, router_weight, gate_weight, up_weight, down_weight = weights
    count = rows.shape[0]
    groups = HEADS // KV_HEADS
    scale = HEAD_DIM ** (-0.5)
    half = HEAD_DIM // 2
    freqs = 10000.0 ** (-jnp.arange(half, dtype=jnp.float32) / half)
    angle = inner.astype(jnp.float32)[:, None] * freqs[None, :]
    cosine = jnp.cos(angle)[:, None, :]
    sine = jnp.sin(angle)[:, None, :]
    normed = low(rms_norm(rows, attn_gain))
    query = low(rotate(low_back(matmul(normed, query_weight)).reshape(count, HEADS, HEAD_DIM), cosine, sine))
    keys = low(rotate(low_back(matmul(normed, key_weight)).reshape(count, KV_HEADS, HEAD_DIM), cosine, sine))
    values = low(low_back(matmul(normed, value_weight))).reshape(count, KV_HEADS, HEAD_DIM)
    allowed = (docs[None, :] == docs[:, None]) & (places[None, :] <= places[:, None])

    def attend(pieces):
        query_group, key_head, value_head = pieces
        scores = low_back(jnp.einsum('tgd,sd->gts', query_group, key_head, precision=lax.Precision.HIGHEST) * scale)
        masked = jnp.where(allowed[None], scores, NEGATIVE)
        probs = jax.nn.softmax(masked, axis=-1)
        return jnp.einsum('gts,sd->tgd', low(probs), value_head, precision=lax.Precision.HIGHEST)
    stacked = (jnp.transpose(query.reshape(count, KV_HEADS, groups, HEAD_DIM), (1, 0, 2, 3)), jnp.transpose(keys, (1, 0, 2)), jnp.transpose(values, (1, 0, 2)))
    mixed = lax.map(jax.checkpoint(attend), stacked)
    attended = low(low_back(jnp.transpose(mixed, (1, 0, 2, 3)).reshape(count, HEADS * HEAD_DIM)))
    resid = rows + low_back(matmul(attended, output_weight.T))
    normed_two = low(rms_norm(resid, ffn_gain))
    logits = matmul(normed_two, router_weight)
    onehot = (route_rows[:, :, None] == jnp.arange(EXPERTS, dtype=jnp.int32)[None, None, :]).astype(jnp.float32)
    chosen = lax.optimization_barrier(jnp.sum(onehot * logits[:, None, :], axis=2))
    gates = jax.nn.softmax(chosen, axis=1)
    dense = lax.optimization_barrier(jnp.sum(onehot * gates[:, :, None], axis=1))
    gate_pre = low_back(jnp.einsum('td,efd->tef', normed_two, gate_weight, precision=lax.Precision.HIGHEST))
    up_pre = low_back(jnp.einsum('td,efd->tef', normed_two, up_weight, precision=lax.Precision.HIGHEST))
    scaled = low(jax.nn.silu(gate_pre) * up_pre * dense[:, :, None])
    return resid + jnp.einsum('tef,efd->td', scaled, down_weight, precision=lax.Precision.HIGHEST)

def reference(inputs, cotangent, routes, seq_lengths, block_order, attn_gain, query_weight, key_weight, value_weight, output_weight, ffn_gain, router_weight, gate_weight, up_weight, down_weight):
    weights = tuple((item.astype(jnp.float32) for item in (attn_gain, query_weight, key_weight, value_weight, output_weight, ffn_gain, router_weight, gate_weight, up_weight, down_weight)))

    def per_group(totals, pieces):
        rows, grad_rows, route_rows, length_row, order_row = pieces
        places, docs, inner = stream_places(order_row, length_row)

        def forward(weights_in, rows_in):
            return group_forward(weights_in, rows_in, places, docs, inner, route_rows)
        result, pullback = jax.vjp(forward, weights, rows.astype(jnp.float32))
        weight_grads, row_grads = pullback(grad_rows.astype(jnp.float32))
        totals = jax.tree.map(lambda first, second: first + second, totals, weight_grads)
        return (totals, (result.astype(jnp.bfloat16), row_grads))
    zeros = jax.tree.map(jnp.zeros_like, weights)
    stacked = (inputs.reshape(N_DP, GROUP, D), cotangent.reshape(N_DP, GROUP, D), routes.reshape(N_DP, GROUP, TOPK), seq_lengths, block_order)
    totals, (result, row_grads) = lax.scan(per_group, zeros, stacked)
    return (result.reshape(TOKENS, D), row_grads.reshape(TOKENS, D), totals[0], totals[1], totals[2], totals[3], totals[4], totals[5], totals[6], totals[7], totals[8], totals[9])
```

```python
import functools

import jax
import jax.numpy as jnp
from jax import lax
from jax.experimental import pallas as pl
from jax.experimental.pallas import tpu as pltpu
from jax.sharding import PartitionSpec as P

HEADS = 16
KV_HEADS = 8
HEAD_DIM = 64
BLOCK = 64
ROWS = 384
WIDTH = 1024
CHUNK = 256
SLOTS = 6
N_CTX = 4
N_DP = 4
N_TP = 8
PART = ROWS // N_TP
EXPERTS = 32
HALF_EXPERTS = 16
UNITS = 64
HIDDEN = HALF_EXPERTS * UNITS
STEP_ROWS = 256
VMEM = 56 * 1024 * 1024

EPSILON = 1e-05
NEGATIVE = -1e30
SCALE = HEAD_DIM**-0.5
LOW = jnp.bfloat16
WIDE = jnp.float32


def dot_nn(left, right):
    return lax.dot_general(left, right, (((1,), (0,)), ((), ())), preferred_element_type=WIDE)


def dot_nt(left, right):
    return lax.dot_general(left, right, (((1,), (1,)), ((), ())), preferred_element_type=WIDE)


def dot_tn(left, right):
    return lax.dot_general(left, right, (((0,), (0,)), ((), ())), preferred_element_type=WIDE)


def turn(values, start):
    return lax.dynamic_slice_in_dim(
        jnp.concatenate([values, values], axis=1), start, values.shape[1], axis=1
    )


def from_dp(values, k):
    return lax.ppermute(values, "dp", [(s, (s - k) % N_DP) for s in range(N_DP)])


def to_dp(values, k):
    return lax.ppermute(values, "dp", [(s, (s + k) % N_DP) for s in range(N_DP)])


def swap_ctx(values, bit):
    return lax.ppermute(values, "ctx", [(s, s ^ bit) for s in range(N_CTX)])


def scatter_tp(values):
    width = values.shape[1]
    got = lax.all_to_all(values, "tp", 0, 0, tiled=True)
    return jnp.sum(got.reshape(N_TP, PART, width).astype(WIDE), axis=0)


def gather_tp(values):
    return lax.all_to_all(jnp.tile(values, (N_TP, 1)), "tp", 0, 0, tiled=True)


def split_heads(values):
    return jnp.concatenate([values[:, :HEAD_DIM], values[:, HEAD_DIM:]], axis=0)


def join_heads(values):
    return jnp.concatenate([values[:BLOCK], values[BLOCK:]], axis=1)


def attend_kernel(q_ref, kv_ref, first_ref, last_ref, place_ref, out_w_ref, att_ref, sum_ref, *rest):
    probs_refs, (k_ref, v_ref) = rest[:SLOTS], rest[SLOTS:]
    for j in range(SLOTS):
        for c in range(N_CTX):
            rows = kv_ref[c * ROWS + j * BLOCK : c * ROWS + (j + 1) * BLOCK, :]
            at = (j * N_CTX + c) * BLOCK
            k_ref[at : at + BLOCK, :] = rows[:, :HEAD_DIM]
            v_ref[at : at + BLOCK, :] = rows[:, HEAD_DIM:]
    for j in range(SLOTS):
        rows = slice(j * BLOCK, (j + 1) * BLOCK)
        keys = (j + 1) * N_CTX * BLOCK
        query = split_heads(q_ref[rows, :])
        scores = dot_nt(query, k_ref[:keys, :]) * SCALE
        places = place_ref[:, :keys]
        kept = (places >= first_ref[rows, :]) & (places <= last_ref[rows, :])
        kept = jnp.concatenate([kept, kept], axis=0)
        scores = jnp.where(kept, scores, NEGATIVE)
        peak = jnp.max(scores, axis=1, keepdims=True)
        expo = jnp.exp(scores - peak)
        total = jnp.sum(expo, axis=1, keepdims=True)
        probs = (expo * (1.0 / total)).astype(LOW)
        probs_refs[j][...] = probs
        mixed = dot_nn(probs, v_ref[:keys, :]).astype(LOW)
        att_ref[rows, :] = join_heads(mixed)
    sum_ref[...] = dot_nn(att_ref[...], out_w_ref[...]).astype(LOW)


def attend_back_kernel(q_ref, kv_ref, dres_ref, out_w_ref, *rest):
    probs_refs = rest[:SLOTS]
    dq_ref, dkv_ref, k_ref, v_ref, dk_ref, dv_ref, datt_ref = rest[SLOTS:]
    datt_ref[...] = dot_nt(dres_ref[...], out_w_ref[...]).astype(LOW)
    for j in range(SLOTS):
        for c in range(N_CTX):
            rows = kv_ref[c * ROWS + j * BLOCK : c * ROWS + (j + 1) * BLOCK, :]
            at = (j * N_CTX + c) * BLOCK
            k_ref[at : at + BLOCK, :] = rows[:, :HEAD_DIM]
            v_ref[at : at + BLOCK, :] = rows[:, HEAD_DIM:]
    for j in reversed(range(SLOTS)):
        rows = slice(j * BLOCK, (j + 1) * BLOCK)
        keys = (j + 1) * N_CTX * BLOCK
        query = split_heads(q_ref[rows, :])
        dmix = split_heads(datt_ref[rows, :])
        probs = probs_refs[j][...]
        wide = probs.astype(WIDE)
        dprobs = dot_nt(dmix, v_ref[:keys, :])
        delta = jnp.sum(wide * dprobs, axis=1, keepdims=True)
        dscores = (wide * (dprobs - delta)).astype(LOW)
        dq_ref[rows, :] = join_heads(dot_nn(dscores, k_ref[:keys, :]) * SCALE)
        dk = dot_tn(dscores, query) * SCALE
        dv = dot_tn(probs, dmix)
        if j == SLOTS - 1:
            dk_ref[...] = dk
            dv_ref[...] = dv
        else:
            dk_ref[:keys, :] += dk
            dv_ref[:keys, :] += dv
    for j in range(SLOTS):
        for c in range(N_CTX):
            at = (j * N_CTX + c) * BLOCK
            dkv_ref[c * ROWS + j * BLOCK : c * ROWS + (j + 1) * BLOCK, :] = jnp.concatenate(
                [dk_ref[at : at + BLOCK, :], dv_ref[at : at + BLOCK, :]], axis=1
            ).astype(LOW)


def expert_kernel(core_ref, x_ref, dy_ref, named_ref, router_ref, *rest):
    weights, rest = rest[:12], rest[12:]
    (dense_ref, dx_own_ref, dx_far_ref, y_own_ref, y_far_ref), rest = rest[:5], rest[5:]
    grads, (dx_acc, y_acc, dd_acc) = rest[:4], rest[4:]
    step = pl.program_id(0)
    steps = pl.num_programs(0)

    @pl.when(step == 0)
    def _():
        logits = dot_nt(x_ref[...], router_ref[...])
        named = named_ref[...] > 0.5
        logits = jnp.where(named, logits, NEGATIVE)
        peak = jnp.max(logits, axis=1, keepdims=True)
        expo = jnp.where(named, jnp.exp(logits - peak), 0.0)
        dense_ref[...] = expo / jnp.sum(expo, axis=1, keepdims=True)
        dx_acc[...] = jnp.zeros_like(dx_acc)
        y_acc[...] = jnp.zeros_like(y_acc)
        dd_acc[...] = jnp.zeros_like(dd_acc)

    x = x_ref[...]
    dy = dy_ref[...]
    gate_w, up_w, down_w = (
        jnp.concatenate([weights[m * 4 + k][0] for k in range(4)], axis=1) for m in range(3)
    )
    first = core_ref[0] * HALF_EXPERTS + step * (STEP_ROWS // UNITS)
    expert = lax.broadcasted_iota(jnp.int32, (EXPERTS, STEP_ROWS), 0)
    unit = lax.broadcasted_iota(jnp.int32, (EXPERTS, STEP_ROWS), 1)
    spread = (expert == first + unit // UNITS).astype(WIDE)
    dense = lax.dot_general(
        dense_ref[...],
        spread,
        (((1,), (0,)), ((), ())),
        precision=lax.Precision.HIGHEST,
        preferred_element_type=WIDE,
    )
    gate_pre = dot_nt(x, gate_w)
    up_pre = dot_nt(x, up_w)
    dscaled = dot_nt(dy, down_w)
    sigmoid = 1.0 / (1.0 + jnp.exp(-gate_pre))
    silu = gate_pre * sigmoid
    active = silu * up_pre
    scaled = (active * dense).astype(LOW)
    dd_acc[...] += dot_nt((dscaled * active).astype(LOW), spread.astype(LOW))
    dactive = dscaled * dense
    dgate = (dactive * up_pre * sigmoid * (1.0 + gate_pre * (1.0 - sigmoid))).astype(LOW)
    dup = (dactive * silu).astype(LOW)
    y_acc[...] += dot_nn(scaled, down_w)
    dx_acc[...] += dot_nn(dgate, gate_w) + dot_nn(dup, up_w)
    for m, (left, right) in enumerate(((dgate, x), (dup, x), (scaled, dy))):
        product = dot_tn(left, right).astype(LOW)
        for k in range(4):
            grads[k][m] = product[:, k * CHUNK : (k + 1) * CHUNK]

    @pl.when(step == steps - 1)
    def _():
        fill = jnp.zeros((ROWS, 128 - EXPERTS), LOW)
        y_own_ref[...] = y_acc[:ROWS, :].astype(LOW)
        y_far_ref[...] = y_acc[ROWS:, :].astype(LOW)
        dx_own_ref[:, :WIDTH] = dx_acc[:ROWS, :].astype(LOW)
        dx_own_ref[:, WIDTH:] = jnp.concatenate([dd_acc[:ROWS, :].astype(LOW), fill], axis=1)
        dx_far_ref[:, :WIDTH] = dx_acc[ROWS:, :].astype(LOW)
        dx_far_ref[:, WIDTH:] = jnp.concatenate([dd_acc[ROWS:, :].astype(LOW), fill], axis=1)


def attend(query, kv, first, last, places, out_w):
    shapes = [
        jax.ShapeDtypeStruct((ROWS, 128), LOW),
        jax.ShapeDtypeStruct((ROWS, WIDTH), LOW),
    ] + [
        jax.ShapeDtypeStruct((2 * BLOCK, (j + 1) * N_CTX * BLOCK), LOW) for j in range(SLOTS)
    ]
    return pl.pallas_call(
        attend_kernel,
        out_shape=shapes,
        scratch_shapes=[pltpu.VMEM((N_CTX * ROWS, HEAD_DIM), LOW)] * 2,
        compiler_params=pltpu.CompilerParams(vmem_limit_bytes=VMEM),
        name="attend",
    )(query, kv, first, last, places, out_w)


def attend_back(query, kv, dresid, out_w, probs):
    return pl.pallas_call(
        attend_back_kernel,
        out_shape=[
            jax.ShapeDtypeStruct((ROWS, 128), WIDE),
            jax.ShapeDtypeStruct((N_CTX * ROWS, 128), LOW),
        ],
        scratch_shapes=[pltpu.VMEM((N_CTX * ROWS, HEAD_DIM), LOW)] * 2
        + [pltpu.VMEM((N_CTX * ROWS, HEAD_DIM), WIDE)] * 2
        + [pltpu.VMEM((ROWS, 128), LOW)],
        compiler_params=pltpu.CompilerParams(vmem_limit_bytes=VMEM),
        name="attend_back",
    )(query, kv, dresid, out_w, *probs)


def experts(core, x, dy, named, router, pieces):
    whole = lambda shape: pl.BlockSpec(shape, lambda i: (0,) * len(shape))
    rows = x.shape[0]
    weight_specs = [
        pl.BlockSpec((1, STEP_ROWS, CHUNK), functools.partial(lambda m, i: (m, i, 0), m))
        for m in range(3)
        for _ in range(4)
    ]
    return pl.pallas_call(
        expert_kernel,
        grid=(HIDDEN // STEP_ROWS,),
        in_specs=[
            pl.BlockSpec(memory_space=pltpu.SMEM),
            whole((rows, WIDTH)),
            whole((rows, WIDTH)),
            whole((rows, EXPERTS)),
            whole((EXPERTS, WIDTH)),
        ]
        + weight_specs,
        out_specs=[
            whole((rows, EXPERTS)),
            whole((ROWS, WIDTH + 128)),
            whole((ROWS, WIDTH + 128)),
            whole((ROWS, WIDTH)),
            whole((ROWS, WIDTH)),
        ]
        + [pl.BlockSpec((3, STEP_ROWS, CHUNK), lambda i: (0, i, 0))] * 4,
        out_shape=[
            jax.ShapeDtypeStruct((rows, EXPERTS), WIDE),
            jax.ShapeDtypeStruct((ROWS, WIDTH + 128), LOW),
            jax.ShapeDtypeStruct((ROWS, WIDTH + 128), LOW),
            jax.ShapeDtypeStruct((ROWS, WIDTH), LOW),
            jax.ShapeDtypeStruct((ROWS, WIDTH), LOW),
        ]
        + [jax.ShapeDtypeStruct((3, HIDDEN, CHUNK), LOW)] * 4,
        scratch_shapes=[
            pltpu.VMEM((rows, WIDTH), WIDE),
            pltpu.VMEM((rows, WIDTH), WIDE),
            pltpu.VMEM((rows, EXPERTS), WIDE),
        ],
        compiler_params=pltpu.CompilerParams(
            vmem_limit_bytes=VMEM, dimension_semantics=("arbitrary",)
        ),
        name="experts",
    )(core, x, dy, named, router, *[pieces[k] for _ in range(3) for k in range(4)])


def swap_rows(weight):
    parts = []
    for at in range(0, weight.shape[0], HEAD_DIM):
        half = HEAD_DIM // 2
        parts += [-weight[at + half : at + HEAD_DIM], weight[at : at + half]]
    return jnp.concatenate(parts, axis=0)


def unrotate(values, cosine, sine):
    half = HEAD_DIM // 2
    parts = []
    for at in range(0, values.shape[1], HEAD_DIM):
        a = values[:, at : at + half]
        b = values[:, at + half : at + HEAD_DIM]
        parts += [a * cosine + b * sine, b * cosine - a * sine]
    return jnp.concatenate(parts, axis=1)


def body(
    inputs,
    cotangent,
    routes,
    seq_lengths,
    block_order,
    attn_gain,
    query_weight,
    key_weight,
    value_weight,
    output_weight,
    ffn_gain,
    router_weight,
    gate_weight,
    up_weight,
    down_weight,
):
    dp = lax.axis_index("dp")
    ctx = lax.axis_index("ctx")
    tp = lax.axis_index("tp")
    core = ctx % 2

    small = jnp.concatenate(
        [
            query_weight.T,
            key_weight.T,
            value_weight.T,
            output_weight.T,
            router_weight.T,
            attn_gain[None],
            ffn_gain[None],
            jnp.zeros((14, CHUNK), LOW),
        ],
        axis=0,
    )
    small_parts = [small] + [from_dp(small, k) for k in (1, 2, 3)]
    wide_small = jnp.concatenate(small_parts, axis=1)
    qkv_w = wide_small[:256]
    out_w = wide_small[256:384]
    router_w = wide_small[384:416]
    gain_one = wide_small[416:417].astype(WIDE)
    gain_two = wide_small[417:418].astype(WIDE)

    stacked = jnp.stack(
        [
            lax.dynamic_slice_in_dim(w, core * HALF_EXPERTS, HALF_EXPERTS, axis=0).reshape(
                HIDDEN, CHUNK
            )
            for w in (gate_weight, up_weight, down_weight)
        ]
    )
    stacked, _ = lax.optimization_barrier((stacked, small_parts[1:]))
    pieces = [stacked] + [from_dp(stacked, k) for k in (1, 2, 3)]

    rows_low = turn(inputs, dp * CHUNK)
    grad_low = turn(cotangent, dp * CHUNK)
    named = jnp.sum(
        (routes[:, :, None] == jnp.arange(EXPERTS, dtype=jnp.int32)[None, None, :]).astype(WIDE),
        axis=1,
    ).astype(LOW)
    grad_both = jnp.concatenate([grad_low, swap_ctx(grad_low, 1)], axis=0)
    named_both = jnp.concatenate([named, swap_ctx(named, 1)], axis=0).astype(WIDE)

    order = block_order[0]
    offsets = jnp.arange(BLOCK, dtype=jnp.int32)
    mine = lax.dynamic_slice_in_dim(order, ctx * SLOTS, SLOTS)
    my_places = (mine[:, None] * BLOCK + offsets[None, :]).reshape(ROWS, 1)
    lengths = seq_lengths[0]
    ends = jnp.cumsum(lengths)
    passed = (my_places >= ends[None, :]).astype(jnp.int32)
    my_first = jnp.sum(passed * lengths[None, :], axis=1, keepdims=True)
    inner = (my_places - my_first).astype(WIDE)
    by_slot = order.reshape(N_CTX, SLOTS).T.reshape(-1)
    key_places = (by_slot[:, None] * BLOCK + offsets[None, :]).reshape(1, N_CTX * ROWS)
    half = HEAD_DIM // 2
    freqs = 10000.0 ** (-jnp.arange(half, dtype=WIDE) / half)
    angle = inner * freqs[None, :]
    cosine = jnp.cos(angle)
    sine = jnp.sin(angle)
    cos_six = jnp.concatenate([cosine] * 6, axis=1)
    sin_six = jnp.concatenate([sine] * 6, axis=1)

    rows_wide = rows_low.astype(WIDE)
    inv_one = lax.rsqrt(jnp.mean(rows_wide * rows_wide, axis=1, keepdims=True) + EPSILON)
    normed = (rows_wide * inv_one * gain_one).astype(LOW)
    lin = dot_nt(normed, jnp.concatenate([qkv_w, swap_rows(qkv_w[:192])], axis=0))
    rot = (lin[:, :192] * cos_six + lin[:, 256:] * sin_six).astype(LOW)
    query = rot[:, :128]
    kv = jnp.concatenate([rot[:, 128:], lin[:, 192:256].astype(LOW)], axis=1)
    kv_all = lax.all_gather(kv, "ctx", axis=0, tiled=True)
    attended, attn_part, *probs = attend(query, kv_all, my_first, my_places, key_places, out_w)

    attn_sum = scatter_tp(attn_part)
    rows_part = lax.dynamic_slice_in_dim(rows_low, tp * PART, PART).astype(WIDE)
    grad_part = lax.dynamic_slice_in_dim(grad_low, tp * PART, PART).astype(WIDE)
    resid = rows_part + attn_sum
    inv_two = lax.rsqrt(jnp.mean(resid * resid, axis=1, keepdims=True) + EPSILON)
    normed_two = gather_tp((resid * inv_two * gain_two).astype(LOW))
    normed_both = jnp.concatenate([normed_two, swap_ctx(normed_two, 1)], axis=0)

    dense, dx_own, dx_far, y_own, y_far, *grads = experts(
        core.reshape(1).astype(jnp.int32), normed_both, grad_both, named_both, router_w, pieces
    )
    dx = (dx_own.astype(WIDE) + swap_ctx(dx_far, 1).astype(WIDE)).astype(LOW)
    y = (y_own.astype(WIDE) + swap_ctx(y_far, 1).astype(WIDE)).astype(LOW)
    both = scatter_tp(jnp.concatenate([dx, y], axis=1))
    block_part = (resid + both[:, WIDTH + 128 :]).astype(LOW)
    ddense = both[:, WIDTH : WIDTH + EXPERTS]
    dense_part = lax.dynamic_slice_in_dim(dense, tp * PART, PART)
    dlogits = dense_part * (ddense - jnp.sum(dense_part * ddense, axis=1, keepdims=True))
    dnorm_two = both[:, :WIDTH] + jnp.dot(
        dlogits, router_w.astype(WIDE), precision=lax.Precision.HIGHEST
    )
    weighted = dnorm_two * gain_two
    gain_two_part = jnp.sum(dnorm_two * resid * inv_two, axis=0)
    dresid = (
        grad_part
        + inv_two * weighted
        - resid * inv_two**3 * jnp.mean(weighted * resid, axis=1, keepdims=True)
    )
    extra = jnp.concatenate(
        [
            dlogits,
            jnp.pad(gain_two_part.reshape(32, 32), ((0, PART - 32), (0, 0))),
            jnp.zeros((PART, 64), WIDE),
        ],
        axis=1,
    )
    back = gather_tp(jnp.concatenate([dresid, extra], axis=1).astype(LOW))
    dresid_low = back[:, :WIDTH]
    dlogits_low = back[:, WIDTH : WIDTH + 32]
    gain_two_sum = jnp.sum(
        back[:, WIDTH + 32 : WIDTH + 64].reshape(N_TP, PART, 32)[:, :32].astype(WIDE), axis=0
    ).reshape(1, WIDTH)

    dq, dkv = attend_back(query, kv_all, dresid_low, out_w, probs)
    dkv_mine = jnp.sum(
        lax.all_to_all(dkv, "ctx", 0, 0, tiled=True).reshape(N_CTX, ROWS, 128).astype(WIDE), axis=0
    )
    dlin = jnp.concatenate(
        [
            unrotate(jnp.concatenate([dq, dkv_mine[:, :64]], axis=1), cosine, sine),
            dkv_mine[:, 64:],
        ],
        axis=1,
    ).astype(LOW)
    dnorm_one = dot_nn(dlin, qkv_w)
    gain_one_part = jnp.sum(dnorm_one * rows_wide * inv_one, axis=0)

    small_grads = jnp.concatenate(
        [
            dot_tn(dlin, normed).astype(LOW),
            dot_tn(attended, dresid_low).astype(LOW),
            dot_tn(dlogits_low, normed_two).astype(LOW),
            jnp.pad(gain_two_sum.astype(LOW), ((0, 15), (0, 0))),
        ],
        axis=0,
    )
    small_sum = small_grads[:, :CHUNK].astype(WIDE)
    for k in (1, 2, 3):
        small_sum += to_dp(small_grads[:, k * CHUNK : (k + 1) * CHUNK], k).astype(WIDE)
    small_sum = small_sum.astype(LOW)
    small_sum = (small_sum.astype(WIDE) + swap_ctx(small_sum, 1).astype(WIDE)).astype(LOW)
    small_sum = small_sum.astype(WIDE) + swap_ctx(small_sum, 2).astype(WIDE)

    expert_sum = grads[0].astype(WIDE)
    for k in (1, 2, 3):
        expert_sum += to_dp(grads[k], k).astype(WIDE)
    expert_sum = expert_sum.astype(LOW)
    expert_sum = (expert_sum.astype(WIDE) + swap_ctx(expert_sum, 2).astype(WIDE)).astype(LOW)
    expert_far = swap_ctx(expert_sum, 1)
    lower = jnp.where(core == 0, expert_sum, expert_far)
    upper = jnp.where(core == 0, expert_far, expert_sum)
    expert_grads = [
        jnp.concatenate([lower[m], upper[m]], axis=0)
        .astype(WIDE)
        .reshape(EXPERTS, UNITS, CHUNK)
        for m in range(3)
    ]

    tail = jnp.concatenate(
        [
            dnorm_one.astype(LOW),
            jnp.tile(
                jnp.pad(gain_one_part.astype(LOW).reshape(32, 32), ((0, PART - 32), (0, 96))),
                (N_TP, 1),
            ),
        ],
        axis=1,
    )
    tail = scatter_tp(tail)
    gain_one_sum = tail[:32, WIDTH : WIDTH + 32].astype(LOW).reshape(1, WIDTH)
    gain_one_rows = jnp.repeat(
        turn(gain_one_sum, (N_DP - dp) * CHUNK).reshape(N_DP, CHUNK), N_CTX, axis=0
    )
    gain_one_grad = jnp.sum(
        lax.all_to_all(gain_one_rows, ("dp", "ctx"), 0, 0, tiled=True).astype(WIDE), axis=0
    )

    dnorm_part = tail[:, :WIDTH]
    inv_part = lax.dynamic_slice_in_dim(inv_one, tp * PART, PART)
    weighted_one = dnorm_part * gain_one
    input_part = (
        dresid
        + inv_part * weighted_one
        - rows_part * inv_part**3 * jnp.mean(weighted_one * rows_part, axis=1, keepdims=True)
    )
    home = (N_DP - dp) * CHUNK
    last = gather_tp(
        jnp.concatenate([turn(input_part.astype(LOW), home), turn(block_part, home)], axis=1)
    )
    return (
        last[:, WIDTH:],
        last[:, :WIDTH].astype(WIDE),
        gain_one_grad,
        small_sum[:128].T,
        small_sum[128:192].T,
        small_sum[192:256].T,
        small_sum[256:384].T,
        small_sum[416],
        small_sum[384:416].T,
        *expert_grads,
    )


def solution(mesh):
    placed = (
        P(("dp", "ctx"), None),
        P(("dp", "ctx"), None),
        P(("dp", "ctx"), None),
        P("dp", None),
        P("dp", None),
        P("dp"),
        P("dp", "tp"),
        P("dp", "tp"),
        P("dp", "tp"),
        P("dp", "tp"),
        P("dp"),
        P("dp", None),
        P(None, "tp", "dp"),
        P(None, "tp", "dp"),
        P(None, "tp", "dp"),
    )
    return jax.shard_map(
        body,
        mesh=mesh,
        in_specs=placed,
        out_specs=(
            P(("dp", "ctx"), None),
            P(("dp", "ctx"), None),
            P("dp"),
            P("dp", "tp"),
            P("dp", "tp"),
            P("dp", "tp"),
            P("dp", "tp"),
            P("dp"),
            P("dp", None),
            P(None, "tp", "dp"),
            P(None, "tp", "dp"),
            P(None, "tp", "dp"),
        ),
        check_vma=False,
    )
```

```python
import functools

import jax
import jax.numpy as jnp
from jax import lax
from jax.experimental import pallas as pl
from jax.experimental.pallas import tpu as pltpu
from jax.sharding import PartitionSpec as P

HEADS = 16
KV_HEADS = 8
HEAD_DIM = 64
BLOCK = 64
ROWS = 384
WIDTH = 1024
CHUNK = 256
SLOTS = 6
N_CTX = 4
N_DP = 4
N_TP = 8
PART = ROWS // N_TP
EXPERTS = 32
HALF_EXPERTS = 16
UNITS = 64
HIDDEN = HALF_EXPERTS * UNITS
STEP_ROWS = 256
QKV_ROWS = 256
ROPED = 192
ROUTER_ROW = 384
GAIN_ROW = 416
PACK_ROWS = 432
VMEM = 56 * 1024 * 1024

EPSILON = 1e-05
NEGATIVE = -1e30
SCALE = HEAD_DIM**-0.5
LOW = jnp.bfloat16
WIDE = jnp.float32


def dot_nn(left, right):
    return lax.dot_general(left, right, (((1,), (0,)), ((), ())), preferred_element_type=WIDE)


def dot_nt(left, right):
    return lax.dot_general(left, right, (((1,), (1,)), ((), ())), preferred_element_type=WIDE)


def dot_tn(left, right):
    return lax.dot_general(left, right, (((0,), (0,)), ((), ())), preferred_element_type=WIDE)


def turn(values, start):
    return lax.dynamic_slice_in_dim(
        jnp.concatenate([values, values], axis=1), start, values.shape[1], axis=1
    )


def from_dp(values, k):
    return lax.ppermute(values, "dp", [(s, (s - k) % N_DP) for s in range(N_DP)])


def to_dp(values, k):
    return lax.ppermute(values, "dp", [(s, (s + k) % N_DP) for s in range(N_DP)])


def swap_ctx(values, bit):
    return lax.ppermute(values, "ctx", [(s, s ^ bit) for s in range(N_CTX)])


def split_heads(values):
    return jnp.concatenate([values[:, :HEAD_DIM], values[:, HEAD_DIM:]], axis=0)


def join_heads(values):
    return jnp.concatenate([values[:BLOCK], values[BLOCK:]], axis=1)


def attend_kernel(q_ref, kv_ref, first_ref, last_ref, place_ref, out_w_ref, att_ref, sum_ref, *rest):
    probs_refs, (k_ref, v_ref) = rest[:SLOTS], rest[SLOTS:]
    for j in range(SLOTS):
        for c in range(N_CTX):
            rows = kv_ref[c * ROWS + j * BLOCK : c * ROWS + (j + 1) * BLOCK, :]
            at = (j * N_CTX + c) * BLOCK
            k_ref[at : at + BLOCK, :] = rows[:, :HEAD_DIM]
            v_ref[at : at + BLOCK, :] = rows[:, HEAD_DIM:]
    for j in range(SLOTS):
        rows = slice(j * BLOCK, (j + 1) * BLOCK)
        keys = (j + 1) * N_CTX * BLOCK
        query = split_heads(q_ref[rows, :])
        scores = dot_nt(query, k_ref[:keys, :]) * SCALE
        places = place_ref[:, :keys]
        kept = (places >= first_ref[rows, :]) & (places <= last_ref[rows, :])
        kept = jnp.concatenate([kept, kept], axis=0)
        scores = jnp.where(kept, scores, NEGATIVE)
        peak = jnp.max(scores, axis=1, keepdims=True)
        expo = jnp.exp(scores - peak)
        total = jnp.sum(expo, axis=1, keepdims=True)
        probs = (expo * (1.0 / total)).astype(LOW)
        probs_refs[j][...] = probs
        mixed = dot_nn(probs, v_ref[:keys, :]).astype(LOW)
        att_ref[rows, :] = join_heads(mixed)
    sum_ref[...] = dot_nn(att_ref[...], out_w_ref[...]).astype(LOW)


def attend_back_kernel(q_ref, kv_ref, dres_ref, out_w_ref, *rest):
    probs_refs = rest[:SLOTS]
    dq_ref, dkv_ref, k_ref, v_ref, dk_ref, dv_ref, datt_ref = rest[SLOTS:]
    datt_ref[...] = dot_nt(dres_ref[:, :WIDTH], out_w_ref[...]).astype(LOW)
    for j in range(SLOTS):
        for c in range(N_CTX):
            rows = kv_ref[c * ROWS + j * BLOCK : c * ROWS + (j + 1) * BLOCK, :]
            at = (j * N_CTX + c) * BLOCK
            k_ref[at : at + BLOCK, :] = rows[:, :HEAD_DIM]
            v_ref[at : at + BLOCK, :] = rows[:, HEAD_DIM:]
    for j in reversed(range(SLOTS)):
        rows = slice(j * BLOCK, (j + 1) * BLOCK)
        keys = (j + 1) * N_CTX * BLOCK
        query = split_heads(q_ref[rows, :])
        dmix = split_heads(datt_ref[rows, :])
        probs = probs_refs[j][...]
        wide = probs.astype(WIDE)
        dprobs = dot_nt(dmix, v_ref[:keys, :])
        delta = jnp.sum(wide * dprobs, axis=1, keepdims=True)
        dscores = (wide * (dprobs - delta)).astype(LOW)
        dq_ref[rows, :] = join_heads(dot_nn(dscores, k_ref[:keys, :]) * SCALE)
        dk = dot_tn(dscores, query) * SCALE
        dv = dot_tn(probs, dmix)
        if j == SLOTS - 1:
            dk_ref[...] = dk
            dv_ref[...] = dv
        else:
            dk_ref[:keys, :] += dk
            dv_ref[:keys, :] += dv
    for j in range(SLOTS):
        for c in range(N_CTX):
            at = (j * N_CTX + c) * BLOCK
            dkv_ref[c * ROWS + j * BLOCK : c * ROWS + (j + 1) * BLOCK, :] = jnp.concatenate(
                [dk_ref[at : at + BLOCK, :], dv_ref[at : at + BLOCK, :]], axis=1
            ).astype(LOW)


def swap_halves(values):
    half = HEAD_DIM // 2
    parts = []
    for at in range(0, values.shape[1], HEAD_DIM):
        parts += [values[:, at + half : at + HEAD_DIM], values[:, at : at + half]]
    return jnp.concatenate(parts, axis=1)


def project_kernel(x_ref, *rest):
    parts, (cos_ref, sin_ref), outs = rest[:N_DP], rest[N_DP : N_DP + 2], rest[N_DP + 2 :]
    wide_ref, out_w_ref, normed_ref, q_ref, kv_ref = outs
    for k in range(N_DP):
        wide_ref[:, k * CHUNK : (k + 1) * CHUNK] = parts[k][...]
    out_w_ref[...] = wide_ref[QKV_ROWS:ROUTER_ROW, :]
    x = x_ref[...].astype(WIDE)
    inverse = lax.rsqrt(jnp.mean(x * x, axis=1, keepdims=True) + EPSILON)
    gain = wide_ref[GAIN_ROW : GAIN_ROW + 16, :].astype(WIDE)[:1]
    normed = (x * inverse * gain).astype(LOW)
    normed_ref[...] = normed
    lin = dot_nt(normed, wide_ref[:QKV_ROWS, :])
    turned = lin[:, :ROPED] * cos_ref[...] + swap_halves(lin[:, :ROPED]) * sin_ref[...]
    q_ref[...] = turned[:, :128].astype(LOW)
    kv_ref[...] = jnp.concatenate([turned[:, 128:], lin[:, ROPED:]], axis=1).astype(LOW)


def norm_kernel(tp_ref, parts_ref, x_ref, wide_ref, resid_ref, normed_ref):
    at = pl.ds(pl.multiple_of(tp_ref[0] * PART, PART), PART)
    resid = x_ref[at, :].astype(WIDE)
    total = parts_ref[0].astype(WIDE)
    for i in range(1, N_TP):
        total += parts_ref[i].astype(WIDE)
    resid = resid + total
    resid_ref[...] = resid
    gain = wide_ref[GAIN_ROW : GAIN_ROW + 16, :].astype(WIDE)[1:2]
    inverse = lax.rsqrt(jnp.mean(resid * resid, axis=1, keepdims=True) + EPSILON)
    normed = (resid * inverse * gain).astype(LOW)
    for i in range(N_TP):
        normed_ref[i * PART : (i + 1) * PART, :] = normed


def norm_back_kernel(
    tp_ref, parts_ref, resid_ref, dense_ref, dy_ref, wide_ref, dresid_ref, gain_ref, sent_ref
):
    at = pl.ds(pl.multiple_of(tp_ref[0] * PART, PART), PART)
    total = parts_ref[0].astype(WIDE)
    for i in range(1, N_TP):
        total += parts_ref[i].astype(WIDE)
    dense = dense_ref[at, :]
    ddense = total[:, WIDTH : WIDTH + EXPERTS]
    dlogits = dense * (ddense - jnp.sum(dense * ddense, axis=1, keepdims=True))
    dlow = dlogits.astype(LOW)
    drest = (dlogits - dlow.astype(WIDE)).astype(LOW)
    router = wide_ref[ROUTER_ROW : ROUTER_ROW + EXPERTS, :]
    dnorm = total[:, :WIDTH] + dot_nn(dlow, router) + dot_nn(drest, router)
    resid = resid_ref[...]
    inverse = lax.rsqrt(jnp.mean(resid * resid, axis=1, keepdims=True) + EPSILON)
    gain = wide_ref[GAIN_ROW : GAIN_ROW + 16, :].astype(WIDE)[1:2]
    gain_ref[...] = jnp.sum(dnorm * resid * inverse, axis=0, keepdims=True)
    weighted = dnorm * gain
    dresid = (
        dy_ref[at, :].astype(WIDE)
        + inverse * weighted
        - resid * inverse**3 * jnp.mean(weighted * resid, axis=1, keepdims=True)
    )
    dresid_ref[...] = dresid
    sent = jnp.concatenate(
        [dresid.astype(LOW), dlow, jnp.zeros((PART, 128 - EXPERTS), LOW)], axis=1
    )
    for i in range(N_TP):
        sent_ref[i * PART : (i + 1) * PART, :] = sent


def project_back_kernel(
    dq_ref, dkv_ref, cos_ref, sin_ref, normed_ref, x_ref, wide_ref, go_ref, gr_ref, gain_ref,
    dnorm_ref, *chunks
):
    dkv = dkv_ref[0].astype(WIDE)
    for i in range(1, N_CTX):
        dkv += dkv_ref[i].astype(WIDE)
    turned = jnp.concatenate([dq_ref[...], dkv[:, :HEAD_DIM]], axis=1)
    turned = turned * cos_ref[...] - swap_halves(turned) * sin_ref[...]
    dlin = jnp.concatenate([turned, dkv[:, HEAD_DIM:]], axis=1).astype(LOW)
    dnorm = dot_nn(dlin, wide_ref[:QKV_ROWS, :])
    dnorm_ref[:, :WIDTH] = dnorm.astype(LOW)
    x = x_ref[...].astype(WIDE)
    inverse = lax.rsqrt(jnp.mean(x * x, axis=1, keepdims=True) + EPSILON)
    gain_one = jnp.sum(dnorm * (x * inverse), axis=0, keepdims=True)
    extra = [
        part[:, i * 128 : (i + 1) * 128] for part in (gain_one, gain_ref[...]) for i in range(8)
    ]
    extra = jnp.concatenate([*extra, jnp.zeros((PART - 16, 128), WIDE)], axis=0).astype(LOW)
    for i in range(N_TP):
        dnorm_ref[i * PART : (i + 1) * PART, WIDTH:] = extra
    product = dot_tn(dlin, normed_ref[...]).astype(LOW)
    for k in range(N_DP):
        at = slice(k * CHUNK, (k + 1) * CHUNK)
        chunks[k][:QKV_ROWS, :] = product[:, at]
        chunks[k][QKV_ROWS:ROUTER_ROW, :] = go_ref[:, at]
        chunks[k][ROUTER_ROW:GAIN_ROW, :] = gr_ref[:, at]


def last_kernel(at_ref, parts_ref, dresid_ref, x_ref, wide_ref, y_ref, resid_ref, sent_ref, *gains):
    at = pl.ds(pl.multiple_of(at_ref[0] * PART, PART), PART)
    total = parts_ref[0].astype(WIDE)
    for i in range(1, N_TP):
        total += parts_ref[i].astype(WIDE)
    dnorm = total[:, :WIDTH]
    for k in range(N_DP):
        rows = [
            jnp.concatenate([total[r : r + 1, WIDTH:] for r in (2 * k + g, 2 * k + g + 1)], axis=1)
            for g in (0, 8)
        ]
        gains[k][...] = jnp.concatenate([*rows, jnp.zeros((14, CHUNK), WIDE)], axis=0).astype(LOW)
    x = x_ref[at, :].astype(WIDE)
    inverse = lax.rsqrt(jnp.mean(x * x, axis=1, keepdims=True) + EPSILON)
    gain = wide_ref[GAIN_ROW : GAIN_ROW + 16, :].astype(WIDE)[:1]
    weighted = dnorm * gain
    dx = (
        dresid_ref[...]
        + inverse * weighted
        - x * inverse**3 * jnp.mean(weighted * x, axis=1, keepdims=True)
    )
    out = resid_ref[...]
    for i in range(N_TP):
        out += y_ref[i].astype(WIDE)
    home = at_ref[1] * CHUNK
    sent = [pltpu.roll(v, home, 1).astype(LOW) for v in (dx, out)]
    for i in range(N_TP):
        sent_ref[i * PART : (i + 1) * PART, :WIDTH] = sent[0]
        sent_ref[i * PART : (i + 1) * PART, WIDTH:] = sent[1]


def small_kernel(*refs):
    parts, gains, out_ref = refs[:N_DP], refs[N_DP : 2 * N_DP], refs[-1]
    for sources, at in ((parts, slice(0, GAIN_ROW)), (gains, slice(GAIN_ROW, PACK_ROWS))):
        total = sources[0][...].astype(WIDE)
        for ref in sources[1:]:
            total += ref[...].astype(WIDE)
        out_ref[at, :] = total.astype(LOW)


def sum_kernel(count, *refs):
    total = refs[0][...].astype(WIDE)
    for i in range(1, count):
        total += refs[i][...].astype(WIDE)
    refs[-1][...] = total.astype(LOW)


def expert_kernel(core_ref, x_own_ref, x_far_ref, dy_own_ref, dy_far_ref, named_ref, wide_ref, *rest):
    weights, rest = rest[:24], rest[24:]
    (dense_ref, dx_own_ref, dx_far_ref, y_own_ref, y_far_ref), rest = rest[:5], rest[5:]
    grads, (x_ref, dy_ref, dx_acc, y_acc, dd_acc) = rest[:8], rest[8:]
    step = pl.program_id(0)
    steps = pl.num_programs(0)
    early = step < steps // 2

    @pl.when(step == 0)
    def _():
        x_ref[:ROWS, :] = x_own_ref[...]
        x_ref[ROWS:, :] = x_far_ref[...]
        dy_ref[:ROWS, :] = dy_own_ref[...]
        dy_ref[ROWS:, :] = dy_far_ref[...]
        logits = dot_nt(x_ref[...], wide_ref[ROUTER_ROW : ROUTER_ROW + EXPERTS, :])
        named = named_ref[...].astype(WIDE) > 0.5
        logits = jnp.where(named, logits, NEGATIVE)
        peak = jnp.max(logits, axis=1, keepdims=True)
        expo = jnp.where(named, jnp.exp(logits - peak), 0.0)
        dense_ref[...] = expo / jnp.sum(expo, axis=1, keepdims=True)
        dx_acc[...] = jnp.zeros_like(dx_acc)
        y_acc[...] = jnp.zeros_like(y_acc)
        dd_acc[...] = jnp.zeros_like(dd_acc)

    x = x_ref[...]
    dy = dy_ref[...]
    gate_w, up_w, down_w = (
        jnp.concatenate(
            [
                jnp.where(early, weights[m * 8 + k * 2][0], weights[m * 8 + k * 2 + 1][0])
                for k in range(4)
            ],
            axis=1,
        )
        for m in range(3)
    )
    first = core_ref[0] * HALF_EXPERTS + step * (STEP_ROWS // UNITS)
    expert = lax.broadcasted_iota(jnp.int32, (EXPERTS, STEP_ROWS), 0)
    unit = lax.broadcasted_iota(jnp.int32, (EXPERTS, STEP_ROWS), 1)
    spread = (expert == first + unit // UNITS).astype(WIDE)
    dense = lax.dot_general(
        dense_ref[...],
        spread,
        (((1,), (0,)), ((), ())),
        precision=lax.Precision.HIGHEST,
        preferred_element_type=WIDE,
    )
    gate_pre = dot_nt(x, gate_w)
    up_pre = dot_nt(x, up_w)
    dscaled = dot_nt(dy, down_w)
    sigmoid = 1.0 / (1.0 + jnp.exp(-gate_pre))
    silu = gate_pre * sigmoid
    active = silu * up_pre
    scaled = (active * dense).astype(LOW)
    dd_acc[...] += dot_nt((dscaled * active).astype(LOW), spread.astype(LOW))
    dactive = dscaled * dense
    dgate = (dactive * up_pre * sigmoid * (1.0 + gate_pre * (1.0 - sigmoid))).astype(LOW)
    dup = (dactive * silu).astype(LOW)
    y_acc[...] += dot_nn(scaled, down_w)
    dx_acc[...] += dot_nn(dgate, gate_w) + dot_nn(dup, up_w)
    products = [dot_tn(left, right).astype(LOW) for left, right in ((dgate, x), (dup, x), (scaled, dy))]

    def store(half):
        for m in range(3):
            for k in range(4):
                grads[2 * k + half][m] = products[m][:, k * CHUNK : (k + 1) * CHUNK]

    pl.when(early)(functools.partial(store, 0))
    pl.when(jnp.logical_not(early))(functools.partial(store, 1))

    @pl.when(step == steps - 1)
    def _():
        fill = jnp.zeros((ROWS, 128 - EXPERTS), LOW)
        y_own_ref[...] = y_acc[:ROWS, :].astype(LOW)
        y_far_ref[...] = y_acc[ROWS:, :].astype(LOW)
        dx_own_ref[:, :WIDTH] = dx_acc[:ROWS, :].astype(LOW)
        dx_own_ref[:, WIDTH:] = jnp.concatenate([dd_acc[:ROWS, :].astype(LOW), fill], axis=1)
        dx_far_ref[:, :WIDTH] = dx_acc[ROWS:, :].astype(LOW)
        dx_far_ref[:, WIDTH:] = jnp.concatenate([dd_acc[ROWS:, :].astype(LOW), fill], axis=1)


ANY = pl.BlockSpec(memory_space=pl.ANY)
SMEM = pl.BlockSpec(memory_space=pltpu.SMEM)
WHOLE = pl.BlockSpec(memory_space=pltpu.VMEM)


def local_call(kernel, outs, *operands, after=(), scalars=(), name, us=2.0):
    skip = len(after)

    def run(*refs):
        kernel(*refs[skip:])

    return pl.pallas_call(
        run,
        in_specs=[ANY] * skip + [SMEM] * len(scalars) + [WHOLE] * len(operands),
        out_specs=[WHOLE] * len(outs),
        out_shape=[jax.ShapeDtypeStruct(shape, dtype) for shape, dtype in outs],
        compiler_params=pltpu.CompilerParams(vmem_limit_bytes=VMEM),
        cost_estimate=pl.CostEstimate(
            flops=int(us * 1e9), bytes_accessed=int(us * 3e6), transcendentals=0
        ),
        name=name,
    )(*after, *scalars, *operands)


def sum_parts(parts, after=(), name="sum_parts"):
    (total,) = local_call(
        functools.partial(sum_kernel, len(parts)), [(parts[0].shape, LOW)], *parts,
        after=after, name=name,
    )
    return total


def cut_kernel(core_ref, after_ref, gate_ref, up_ref, down_ref, *outs):
    for half in range(2):
        for m, ref in enumerate((gate_ref, up_ref, down_ref)):
            at = half * (HALF_EXPERTS // 2)
            outs[half][m] = ref[at : at + HALF_EXPERTS // 2].reshape(HIDDEN // 2, CHUNK)


def cut_weights(core, weights, after):
    mine = pl.BlockSpec((HALF_EXPERTS, UNITS, CHUNK), lambda i, core_ref: (core_ref[0], 0, 0))
    part = (3, HIDDEN // 2, CHUNK)
    return pl.pallas_call(
        cut_kernel,
        grid_spec=pltpu.PrefetchScalarGridSpec(
            num_scalar_prefetch=1,
            grid=(1,),
            in_specs=[ANY] + [mine] * 3,
            out_specs=[pl.BlockSpec(part, lambda i, core_ref: (0, 0, 0))] * 2,
        ),
        out_shape=[jax.ShapeDtypeStruct(part, LOW)] * 2,
        compiler_params=pltpu.CompilerParams(vmem_limit_bytes=VMEM),
        name="cut_weights",
    )(core, after, *weights)


def place_kernel(core_ref, *refs):
    sources, last_ref, (block_ref, input_ref), outs = refs[:4], refs[4], refs[5:7], refs[7:]
    input_ref[...] = last_ref[:, :WIDTH].astype(WIDE)
    block_ref[...] = last_ref[:, WIDTH:]
    whose, half = pl.program_id(0), pl.program_id(1)
    mine = whose == core_ref[0]
    for h in range(2):
        for own in range(2):

            @pl.when((half == h) & (mine == (own == 1)))
            def _():
                source = sources[2 * h + (0 if own else 1)]
                for m in range(3):
                    outs[m][...] = (
                        source[m].astype(WIDE).reshape(HALF_EXPERTS // 2, UNITS, CHUNK)
                    )


def place_grads(core, sources, last):
    return pl.pallas_call(
        place_kernel,
        grid=(2, 2),
        in_specs=[SMEM]
        + [pl.BlockSpec((3, HIDDEN // 2, CHUNK), lambda i, j: (0, 0, 0))] * 4
        + [pl.BlockSpec((ROWS // 4, 2 * WIDTH), lambda i, j: (2 * i + j, 0))],
        out_specs=[pl.BlockSpec((ROWS // 4, WIDTH), lambda i, j: (2 * i + j, 0))] * 2
        + [pl.BlockSpec((HALF_EXPERTS // 2, UNITS, CHUNK), lambda i, j: (2 * i + j, 0, 0))] * 3,
        out_shape=[
            jax.ShapeDtypeStruct((ROWS, WIDTH), LOW),
            jax.ShapeDtypeStruct((ROWS, WIDTH), WIDE),
        ]
        + [jax.ShapeDtypeStruct((EXPERTS, UNITS, CHUNK), WIDE)] * 3,
        compiler_params=pltpu.CompilerParams(vmem_limit_bytes=VMEM),
        name="place_grads",
    )(core, *sources, last)


def attend(query, kv, first, last, places, out_w, after=()):
    skip = len(after)
    shapes = [
        jax.ShapeDtypeStruct((ROWS, 128), LOW),
        jax.ShapeDtypeStruct((ROWS, WIDTH), LOW),
    ] + [
        jax.ShapeDtypeStruct((2 * BLOCK, (j + 1) * N_CTX * BLOCK), LOW) for j in range(SLOTS)
    ]

    def run(*refs):
        attend_kernel(*refs[skip:])

    return pl.pallas_call(
        run,
        in_specs=[ANY] * skip + [WHOLE] * 6,
        out_specs=[WHOLE] * len(shapes),
        out_shape=shapes,
        cost_estimate=pl.CostEstimate(flops=6 * 10**9, bytes_accessed=10**7, transcendentals=0),
        scratch_shapes=[pltpu.VMEM((N_CTX * ROWS, HEAD_DIM), LOW)] * 2,
        compiler_params=pltpu.CompilerParams(vmem_limit_bytes=VMEM),
        name="attend",
    )(*after, query, kv, first, last, places, out_w)


def attend_back(query, kv, dresid, out_w, probs, after=()):
    skip = len(after)

    def run(*refs):
        attend_back_kernel(*refs[skip:])

    return pl.pallas_call(
        run,
        in_specs=[ANY] * skip + [WHOLE] * (4 + SLOTS),
        out_specs=[WHOLE] * 2,
        cost_estimate=pl.CostEstimate(flops=6 * 10**9, bytes_accessed=10**7, transcendentals=0),
        out_shape=[
            jax.ShapeDtypeStruct((ROWS, 128), WIDE),
            jax.ShapeDtypeStruct((N_CTX * ROWS, 128), LOW),
        ],
        scratch_shapes=[pltpu.VMEM((N_CTX * ROWS, HEAD_DIM), LOW)] * 2
        + [pltpu.VMEM((N_CTX * ROWS, HEAD_DIM), WIDE)] * 2
        + [pltpu.VMEM((ROWS, 128), LOW)],
        compiler_params=pltpu.CompilerParams(vmem_limit_bytes=VMEM),
        name="attend_back",
    )(*after, query, kv, dresid, out_w, *probs)


def experts(core, x_own, x_far, dy_own, dy_far, named, wide, pieces):
    whole = lambda shape: pl.BlockSpec(shape, lambda i: (0,) * len(shape))
    rows = 2 * ROWS
    half_steps = HIDDEN // STEP_ROWS // 2
    weight_specs = [
        pl.BlockSpec((1, STEP_ROWS, CHUNK), functools.partial(index, m))
        for m in range(3)
        for _ in range(4)
        for index in (
            lambda m, i: (m, jnp.minimum(i, half_steps - 1), 0),
            lambda m, i: (m, jnp.maximum(i - half_steps, 0), 0),
        )
    ]
    grad_specs = [
        pl.BlockSpec((3, STEP_ROWS, CHUNK), lambda i: (0, jnp.minimum(i, half_steps - 1), 0)),
        pl.BlockSpec((3, STEP_ROWS, CHUNK), lambda i: (0, jnp.maximum(i - half_steps, 0), 0)),
    ]
    return pl.pallas_call(
        expert_kernel,
        grid=(HIDDEN // STEP_ROWS,),
        in_specs=[SMEM]
        + [whole((ROWS, WIDTH))] * 4
        + [whole((rows, EXPERTS)), whole(wide.shape)]
        + weight_specs,
        out_specs=[
            whole((rows, EXPERTS)),
            whole((ROWS, WIDTH + 128)),
            whole((ROWS, WIDTH + 128)),
            whole((ROWS, WIDTH)),
            whole((ROWS, WIDTH)),
        ]
        + grad_specs * 4,
        out_shape=[
            jax.ShapeDtypeStruct((rows, EXPERTS), WIDE),
            jax.ShapeDtypeStruct((ROWS, WIDTH + 128), LOW),
            jax.ShapeDtypeStruct((ROWS, WIDTH + 128), LOW),
            jax.ShapeDtypeStruct((ROWS, WIDTH), LOW),
            jax.ShapeDtypeStruct((ROWS, WIDTH), LOW),
        ]
        + [jax.ShapeDtypeStruct((3, HIDDEN // 2, CHUNK), LOW)] * 8,
        scratch_shapes=[
            pltpu.VMEM((rows, WIDTH), LOW),
            pltpu.VMEM((rows, WIDTH), LOW),
            pltpu.VMEM((rows, WIDTH), WIDE),
            pltpu.VMEM((rows, WIDTH), WIDE),
            pltpu.VMEM((rows, EXPERTS), WIDE),
        ],
        compiler_params=pltpu.CompilerParams(
            vmem_limit_bytes=VMEM, dimension_semantics=("arbitrary",)
        ),
        cost_estimate=pl.CostEstimate(
            flops=25 * 10**9, bytes_accessed=3 * 10**7, transcendentals=0
        ),
        name="experts",
    )(
        core, x_own, x_far, dy_own, dy_far, named, wide,
        *[pieces[k][half] for _ in range(3) for k in range(4) for half in range(2)],
    )


def body(
    inputs,
    cotangent,
    routes,
    seq_lengths,
    block_order,
    attn_gain,
    query_weight,
    key_weight,
    value_weight,
    output_weight,
    ffn_gain,
    router_weight,
    gate_weight,
    up_weight,
    down_weight,
):
    dp = lax.axis_index("dp")
    ctx = lax.axis_index("ctx")
    tp = lax.axis_index("tp")
    core = ctx % 2

    core_at = core.reshape(1).astype(jnp.int32)
    tp_at = tp.reshape(1).astype(jnp.int32)
    dp_at = dp.reshape(1).astype(jnp.int32)

    small = jnp.concatenate(
        [
            query_weight.T,
            key_weight.T,
            value_weight.T,
            output_weight.T,
            router_weight.T,
            attn_gain[None],
            ffn_gain[None],
            jnp.zeros((14, CHUNK), LOW),
        ],
        axis=0,
    )
    small_parts = [small] + [from_dp(small, k) for k in (1, 2, 3)]

    rows_low = turn(inputs, dp * CHUNK)
    grad_low = turn(cotangent, dp * CHUNK)
    named = jnp.sum(
        (routes[:, :, None] == jnp.arange(EXPERTS, dtype=jnp.int32)[None, None, :]).astype(WIDE),
        axis=1,
    ).astype(LOW)
    grad_far = swap_ctx(grad_low, 1)
    named_both = jnp.concatenate([named, swap_ctx(named, 1)], axis=0)

    order = block_order[0]
    offsets = jnp.arange(BLOCK, dtype=jnp.int32)
    mine = lax.dynamic_slice_in_dim(order, ctx * SLOTS, SLOTS)
    my_places = (mine[:, None] * BLOCK + offsets[None, :]).reshape(ROWS, 1)
    lengths = seq_lengths[0]
    ends = jnp.cumsum(lengths)
    passed = (my_places >= ends[None, :]).astype(jnp.int32)
    my_first = jnp.sum(passed * lengths[None, :], axis=1, keepdims=True)
    inner = (my_places - my_first).astype(WIDE)
    by_slot = order.reshape(N_CTX, SLOTS).T.reshape(-1)
    key_places = (by_slot[:, None] * BLOCK + offsets[None, :]).reshape(1, N_CTX * ROWS)
    half = HEAD_DIM // 2
    freqs = 10000.0 ** (-jnp.arange(half, dtype=WIDE) / half)
    angle = inner * freqs[None, :]
    cosine = jnp.cos(angle)
    sine = jnp.sin(angle)
    cos_six = jnp.concatenate([cosine] * 6, axis=1)
    sin_six = jnp.concatenate([-sine, sine] * 3, axis=1)

    own = cut_weights(core_at, (gate_weight, up_weight, down_weight), small_parts[1])
    right = [from_dp(part, 1) for part in own]
    left = [from_dp(part, 3) for part in own]
    across = [from_dp(right[0], 1), from_dp(left[1], 3)]
    pieces = [own, right, across, left]

    wide, out_w, normed, query, kv = local_call(
        project_kernel,
        [
            ((PACK_ROWS, WIDTH), LOW),
            ((128, WIDTH), LOW),
            ((ROWS, WIDTH), LOW),
            ((ROWS, 128), LOW),
            ((ROWS, 128), LOW),
        ],
        rows_low, *small_parts, cos_six, sin_six,
        name="project",
    )
    kv_all = lax.all_gather(kv, "ctx", axis=0, tiled=True)
    attended, attn_part, *probs = attend(
        query, kv_all, my_first, my_places, key_places, out_w, after=(right[0], left[0])
    )

    attn_parts = lax.all_to_all(attn_part, "tp", 0, 0, tiled=True).reshape(N_TP, PART, WIDTH)
    resid, normed_sent = local_call(
        norm_kernel,
        [((PART, WIDTH), WIDE), ((ROWS, WIDTH), LOW)],
        attn_parts, rows_low, wide,
        scalars=(tp_at,), after=(right[1], left[1]), name="norm",
    )
    normed_two = lax.all_to_all(normed_sent, "tp", 0, 0, tiled=True)
    normed_far = swap_ctx(normed_two, 1)

    dense, dx_own, dx_far, y_own, y_far, *grads = experts(
        core_at, normed_two, normed_far, grad_low, grad_far, named_both, wide, pieces
    )
    chunks = [grads[2 * k : 2 * k + 2] for k in range(4)]

    by_left = to_dp(chunks[2][0], 1)
    by_right = to_dp(chunks[2][1], 3)
    straight = [to_dp(chunks[3][0], 3), to_dp(chunks[1][1], 1)]

    dx = (dx_own.astype(WIDE) + swap_ctx(dx_far, 1).astype(WIDE)).astype(LOW)
    dx_parts = lax.all_to_all(dx, "tp", 0, 0, tiled=True).reshape(N_TP, PART, WIDTH + 128)
    relay_right = sum_parts([chunks[1][0], by_left])
    relay_left = sum_parts([chunks[3][1], by_right])
    dresid, gain_two_part, sent = local_call(
        norm_back_kernel,
        [((PART, WIDTH), WIDE), ((1, WIDTH), WIDE), ((ROWS, WIDTH + 128), LOW)],
        dx_parts, resid, dense, grad_low, wide,
        scalars=(tp_at,), after=(relay_right, relay_left), name="norm_back",
    )
    relayed = [to_dp(relay_right, 1), to_dp(relay_left, 3)]
    first, second = ([chunks[0][h], straight[h], relayed[h]] for h in range(2))
    back = lax.all_to_all(sent, "tp", 0, 0, tiled=True)
    dlogits_low = back[:, WIDTH : WIDTH + EXPERTS]
    first_half = sum_parts(first)
    first_other = swap_ctx(first_half, 2)
    dq, dkv = attend_back(query, kv_all, back, out_w, probs, after=(first_half,))
    y = sum_parts([y_own, swap_ctx(y_far, 1)], after=(dq, first_other))
    y_parts = lax.all_to_all(y, "tp", 0, 0, tiled=True).reshape(N_TP, PART, WIDTH)
    second_half = sum_parts(second, after=(y,))
    second_other = swap_ctx(second_half, 2)
    dkv_parts = lax.all_to_all(dkv, "ctx", 0, 0, tiled=True).reshape(N_CTX, ROWS, 128)
    dnorm_one, *small_chunks = local_call(
        project_back_kernel,
        [((ROWS, WIDTH + 128), LOW)] + [((GAIN_ROW, CHUNK), LOW)] * N_DP,
        dq, dkv_parts, cos_six, sin_six, normed, rows_low, wide,
        dot_tn(attended, back[:, :WIDTH]).astype(LOW),
        dot_tn(dlogits_low, normed_two).astype(LOW),
        gain_two_part,
        after=(second_half,),
        name="project_back", us=4.0,
    )

    dnorm_parts = lax.all_to_all(dnorm_one, "tp", 0, 0, tiled=True).reshape(
        N_TP, PART, WIDTH + 128
    )
    small_parts = [small_chunks[0]] + [to_dp(small_chunks[k], k) for k in (1, 2, 3)]
    sent, *gain_chunks = local_call(
        last_kernel,
        [((ROWS, 2 * WIDTH), LOW)] + [((16, CHUNK), LOW)] * N_DP,
        dnorm_parts, dresid, rows_low, wide, y_parts, resid,
        scalars=(jnp.concatenate([tp_at, dp_at]),), after=tuple(small_parts[1:]),
        name="last",
    )
    last = lax.all_to_all(sent, "tp", 0, 0, tiled=True)
    gain_parts = [gain_chunks[0]] + [to_dp(gain_chunks[k], k) for k in (1, 2, 3)]
    (small_sum,) = local_call(
        small_kernel, [((PACK_ROWS, CHUNK), LOW)], *small_parts, *gain_parts,
        after=(second_other,), name="small"
    )
    small_sum = sum_parts([small_sum, swap_ctx(small_sum, 1)])
    small_sum = small_sum.astype(WIDE) + swap_ctx(small_sum, 2).astype(WIDE)

    first_half = sum_parts([first_half, first_other], after=(sent,))
    second_half = sum_parts([second_half, second_other], after=(last,))
    block_output, input_grad, *expert_grads = place_grads(
        core_at,
        [first_half, swap_ctx(first_half, 1), second_half, swap_ctx(second_half, 1)],
        last,
    )
    return (
        block_output,
        input_grad,
        small_sum[GAIN_ROW],
        small_sum[:128].T,
        small_sum[128:192].T,
        small_sum[192:256].T,
        small_sum[256:384].T,
        small_sum[GAIN_ROW + 1],
        small_sum[384:416].T,
        *expert_grads,
    )


def solution(mesh):
    placed = (
        P(("dp", "ctx"), None),
        P(("dp", "ctx"), None),
        P(("dp", "ctx"), None),
        P("dp", None),
        P("dp", None),
        P("dp"),
        P("dp", "tp"),
        P("dp", "tp"),
        P("dp", "tp"),
        P("dp", "tp"),
        P("dp"),
        P("dp", None),
        P(None, "tp", "dp"),
        P(None, "tp", "dp"),
        P(None, "tp", "dp"),
    )
    return jax.shard_map(
        body,
        mesh=mesh,
        in_specs=placed,
        out_specs=(
            P(("dp", "ctx"), None),
            P(("dp", "ctx"), None),
            P("dp"),
            P("dp", "tp"),
            P("dp", "tp"),
            P("dp", "tp"),
            P("dp", "tp"),
            P("dp"),
            P("dp", None),
            P(None, "tp", "dp"),
            P(None, "tp", "dp"),
            P(None, "tp", "dp"),
        ),
        check_vma=False,
    )
```

```python
import functools

import jax
import jax.numpy as jnp
from jax import lax
from jax.experimental import pallas as pl
from jax.experimental.pallas import tpu as pltpu
from jax.sharding import PartitionSpec as P

HEADS = 16
KV_HEADS = 8
HEAD_DIM = 64
BLOCK = 64
ROWS = 384
WIDTH = 1024
CHUNK = 256
SLOTS = 6
N_CTX = 4
N_DP = 4
N_TP = 8
PART = ROWS // N_TP
EXPERTS = 32
HALF_EXPERTS = 16
UNITS = 64
HIDDEN = HALF_EXPERTS * UNITS
STEP_ROWS = 256
QKV_ROWS = 256
ROPED = 192
ROUTER_ROW = 384
GAIN_ROW = 416
PACK_ROWS = 432
VMEM = 56 * 1024 * 1024

EPSILON = 1e-05
NEGATIVE = -1e30
SCALE = HEAD_DIM**-0.5
LOW = jnp.bfloat16
WIDE = jnp.float32


def dot_nn(left, right):
    return lax.dot_general(left, right, (((1,), (0,)), ((), ())), preferred_element_type=WIDE)


def dot_nt(left, right):
    return lax.dot_general(left, right, (((1,), (1,)), ((), ())), preferred_element_type=WIDE)


def dot_tn(left, right):
    return lax.dot_general(left, right, (((0,), (0,)), ((), ())), preferred_element_type=WIDE)


def turn(values, start):
    return lax.dynamic_slice_in_dim(
        jnp.concatenate([values, values], axis=1), start, values.shape[1], axis=1
    )


def from_dp(values, k):
    return lax.ppermute(values, "dp", [(s, (s - k) % N_DP) for s in range(N_DP)])


def to_dp(values, k):
    return lax.ppermute(values, "dp", [(s, (s + k) % N_DP) for s in range(N_DP)])


def swap_ctx(values, bit):
    return lax.ppermute(values, "ctx", [(s, s ^ bit) for s in range(N_CTX)])


def split_heads(values):
    return jnp.concatenate([values[:, :HEAD_DIM], values[:, HEAD_DIM:]], axis=0)


def join_heads(values):
    return jnp.concatenate([values[:BLOCK], values[BLOCK:]], axis=1)


def attend_kernel(q_ref, kv_ref, first_ref, last_ref, place_ref, out_w_ref, att_ref, sum_ref, *rest):
    probs_refs, (k_ref, v_ref) = rest[:SLOTS], rest[SLOTS:]
    for j in range(SLOTS):
        for c in range(N_CTX):
            rows = kv_ref[c * ROWS + j * BLOCK : c * ROWS + (j + 1) * BLOCK, :]
            at = (j * N_CTX + c) * BLOCK
            k_ref[at : at + BLOCK, :] = rows[:, :HEAD_DIM]
            v_ref[at : at + BLOCK, :] = rows[:, HEAD_DIM:]
    for j in range(SLOTS):
        rows = slice(j * BLOCK, (j + 1) * BLOCK)
        keys = (j + 1) * N_CTX * BLOCK
        query = split_heads(q_ref[rows, :])
        scores = dot_nt(query, k_ref[:keys, :]) * SCALE
        places = place_ref[:, :keys]
        kept = (places >= first_ref[rows, :]) & (places <= last_ref[rows, :])
        kept = jnp.concatenate([kept, kept], axis=0)
        scores = jnp.where(kept, scores, NEGATIVE)
        peak = jnp.max(scores, axis=1, keepdims=True)
        expo = jnp.exp(scores - peak)
        total = jnp.sum(expo, axis=1, keepdims=True)
        probs = (expo * (1.0 / total)).astype(LOW)
        probs_refs[j][...] = probs
        mixed = dot_nn(probs, v_ref[:keys, :]).astype(LOW)
        att_ref[rows, :] = join_heads(mixed)
    sum_ref[...] = dot_nn(att_ref[...], out_w_ref[...]).astype(LOW)


def attend_back_kernel(q_ref, kv_ref, dres_ref, out_w_ref, *rest):
    probs_refs = rest[:SLOTS]
    dq_ref, dkv_ref, k_ref, v_ref, dk_ref, dv_ref, datt_ref = rest[SLOTS:]
    datt_ref[...] = dot_nt(dres_ref[:, :WIDTH], out_w_ref[...]).astype(LOW)
    for j in range(SLOTS):
        for c in range(N_CTX):
            rows = kv_ref[c * ROWS + j * BLOCK : c * ROWS + (j + 1) * BLOCK, :]
            at = (j * N_CTX + c) * BLOCK
            k_ref[at : at + BLOCK, :] = rows[:, :HEAD_DIM]
            v_ref[at : at + BLOCK, :] = rows[:, HEAD_DIM:]
    for j in reversed(range(SLOTS)):
        rows = slice(j * BLOCK, (j + 1) * BLOCK)
        keys = (j + 1) * N_CTX * BLOCK
        query = split_heads(q_ref[rows, :])
        dmix = split_heads(datt_ref[rows, :])
        probs = probs_refs[j][...]
        wide = probs.astype(WIDE)
        dprobs = dot_nt(dmix, v_ref[:keys, :])
        delta = jnp.sum(wide * dprobs, axis=1, keepdims=True)
        dscores = (wide * (dprobs - delta)).astype(LOW)
        dq_ref[rows, :] = join_heads(dot_nn(dscores, k_ref[:keys, :]) * SCALE)
        dk = dot_tn(dscores, query) * SCALE
        dv = dot_tn(probs, dmix)
        if j == SLOTS - 1:
            dk_ref[...] = dk
            dv_ref[...] = dv
        else:
            dk_ref[:keys, :] += dk
            dv_ref[:keys, :] += dv
    for j in range(SLOTS):
        for c in range(N_CTX):
            at = (j * N_CTX + c) * BLOCK
            dkv_ref[c * ROWS + j * BLOCK : c * ROWS + (j + 1) * BLOCK, :] = jnp.concatenate(
                [dk_ref[at : at + BLOCK, :], dv_ref[at : at + BLOCK, :]], axis=1
            ).astype(LOW)


def swap_halves(values):
    half = HEAD_DIM // 2
    parts = []
    for at in range(0, values.shape[1], HEAD_DIM):
        parts += [values[:, at + half : at + HEAD_DIM], values[:, at : at + half]]
    return jnp.concatenate(parts, axis=1)


def project_kernel(x_ref, *rest):
    parts, (cos_ref, sin_ref), outs = rest[:N_DP], rest[N_DP : N_DP + 2], rest[N_DP + 2 :]
    wide_ref, out_w_ref, normed_ref, q_ref, kv_ref = outs
    for k in range(N_DP):
        wide_ref[:, k * CHUNK : (k + 1) * CHUNK] = parts[k][...]
    out_w_ref[...] = wide_ref[QKV_ROWS:ROUTER_ROW, :]
    x = x_ref[...].astype(WIDE)
    inverse = lax.rsqrt(jnp.mean(x * x, axis=1, keepdims=True) + EPSILON)
    gain = wide_ref[GAIN_ROW : GAIN_ROW + 16, :].astype(WIDE)[:1]
    normed = (x * inverse * gain).astype(LOW)
    normed_ref[...] = normed
    lin = dot_nt(normed, wide_ref[:QKV_ROWS, :])
    turned = lin[:, :ROPED] * cos_ref[...] + swap_halves(lin[:, :ROPED]) * sin_ref[...]
    q_ref[...] = turned[:, :128].astype(LOW)
    kv_ref[...] = jnp.concatenate([turned[:, 128:], lin[:, ROPED:]], axis=1).astype(LOW)


def norm_kernel(tp_ref, parts_ref, x_ref, wide_ref, resid_ref, normed_ref):
    at = pl.ds(pl.multiple_of(tp_ref[0] * PART, PART), PART)
    resid = x_ref[at, :].astype(WIDE)
    total = parts_ref[0].astype(WIDE)
    for i in range(1, N_TP):
        total += parts_ref[i].astype(WIDE)
    resid = resid + total
    resid_ref[...] = resid
    gain = wide_ref[GAIN_ROW : GAIN_ROW + 16, :].astype(WIDE)[1:2]
    inverse = lax.rsqrt(jnp.mean(resid * resid, axis=1, keepdims=True) + EPSILON)
    normed = (resid * inverse * gain).astype(LOW)
    for i in range(N_TP):
        normed_ref[i * PART : (i + 1) * PART, :] = normed


def norm_back_kernel(
    tp_ref, parts_ref, resid_ref, dense_ref, dy_ref, wide_ref, dresid_ref, gain_ref, sent_ref
):
    at = pl.ds(pl.multiple_of(tp_ref[0] * PART, PART), PART)
    total = parts_ref[0].astype(WIDE)
    for i in range(1, N_TP):
        total += parts_ref[i].astype(WIDE)
    dense = dense_ref[at, :]
    ddense = total[:, WIDTH : WIDTH + EXPERTS]
    dlogits = dense * (ddense - jnp.sum(dense * ddense, axis=1, keepdims=True))
    dlow = dlogits.astype(LOW)
    drest = (dlogits - dlow.astype(WIDE)).astype(LOW)
    router = wide_ref[ROUTER_ROW : ROUTER_ROW + EXPERTS, :]
    dnorm = total[:, :WIDTH] + dot_nn(dlow, router) + dot_nn(drest, router)
    resid = resid_ref[...]
    inverse = lax.rsqrt(jnp.mean(resid * resid, axis=1, keepdims=True) + EPSILON)
    gain = wide_ref[GAIN_ROW : GAIN_ROW + 16, :].astype(WIDE)[1:2]
    gain_ref[...] = jnp.sum(dnorm * resid * inverse, axis=0, keepdims=True)
    weighted = dnorm * gain
    dresid = (
        dy_ref[at, :].astype(WIDE)
        + inverse * weighted
        - resid * inverse**3 * jnp.mean(weighted * resid, axis=1, keepdims=True)
    )
    dresid_ref[...] = dresid
    sent = jnp.concatenate(
        [dresid.astype(LOW), dlow, jnp.zeros((PART, 128 - EXPERTS), LOW)], axis=1
    )
    for i in range(N_TP):
        sent_ref[i * PART : (i + 1) * PART, :] = sent


def project_back_kernel(
    dq_ref, dkv_ref, cos_ref, sin_ref, normed_ref, x_ref, wide_ref, go_ref, gr_ref, gain_ref,
    dnorm_ref, *chunks
):
    dkv = dkv_ref[0].astype(WIDE)
    for i in range(1, N_CTX):
        dkv += dkv_ref[i].astype(WIDE)
    turned = jnp.concatenate([dq_ref[...], dkv[:, :HEAD_DIM]], axis=1)
    turned = turned * cos_ref[...] - swap_halves(turned) * sin_ref[...]
    dlin = jnp.concatenate([turned, dkv[:, HEAD_DIM:]], axis=1).astype(LOW)
    dnorm = dot_nn(dlin, wide_ref[:QKV_ROWS, :])
    dnorm_ref[:, :WIDTH] = dnorm.astype(LOW)
    x = x_ref[...].astype(WIDE)
    inverse = lax.rsqrt(jnp.mean(x * x, axis=1, keepdims=True) + EPSILON)
    gain_one = jnp.sum(dnorm * (x * inverse), axis=0, keepdims=True)
    extra = [
        part[:, i * 128 : (i + 1) * 128] for part in (gain_one, gain_ref[...]) for i in range(8)
    ]
    extra = jnp.concatenate([*extra, jnp.zeros((PART - 16, 128), WIDE)], axis=0).astype(LOW)
    for i in range(N_TP):
        dnorm_ref[i * PART : (i + 1) * PART, WIDTH:] = extra
    product = dot_tn(dlin, normed_ref[...]).astype(LOW)
    for k in range(N_DP):
        at = slice(k * CHUNK, (k + 1) * CHUNK)
        chunks[k][:QKV_ROWS, :] = product[:, at]
        chunks[k][QKV_ROWS:ROUTER_ROW, :] = go_ref[:, at]
        chunks[k][ROUTER_ROW:GAIN_ROW, :] = gr_ref[:, at]


def last_kernel(at_ref, parts_ref, dresid_ref, x_ref, wide_ref, y_ref, resid_ref, sent_ref, *gains):
    at = pl.ds(pl.multiple_of(at_ref[0] * PART, PART), PART)
    total = parts_ref[0].astype(WIDE)
    for i in range(1, N_TP):
        total += parts_ref[i].astype(WIDE)
    dnorm = total[:, :WIDTH]
    for k in range(N_DP):
        rows = [
            jnp.concatenate([total[r : r + 1, WIDTH:] for r in (2 * k + g, 2 * k + g + 1)], axis=1)
            for g in (0, 8)
        ]
        gains[k][...] = jnp.concatenate([*rows, jnp.zeros((14, CHUNK), WIDE)], axis=0).astype(LOW)
    x = x_ref[at, :].astype(WIDE)
    inverse = lax.rsqrt(jnp.mean(x * x, axis=1, keepdims=True) + EPSILON)
    gain = wide_ref[GAIN_ROW : GAIN_ROW + 16, :].astype(WIDE)[:1]
    weighted = dnorm * gain
    dx = (
        dresid_ref[...]
        + inverse * weighted
        - x * inverse**3 * jnp.mean(weighted * x, axis=1, keepdims=True)
    )
    out = resid_ref[...]
    for i in range(N_TP):
        out += y_ref[i].astype(WIDE)
    home = at_ref[1] * CHUNK
    sent = [pltpu.roll(v, home, 1).astype(LOW) for v in (dx, out)]
    for i in range(N_TP):
        sent_ref[i * PART : (i + 1) * PART, :WIDTH] = sent[0]
        sent_ref[i * PART : (i + 1) * PART, WIDTH:] = sent[1]


def small_kernel(*refs):
    parts, gains, out_ref = refs[:N_DP], refs[N_DP : 2 * N_DP], refs[-1]
    for sources, at in ((parts, slice(0, GAIN_ROW)), (gains, slice(GAIN_ROW, PACK_ROWS))):
        total = sources[0][...].astype(WIDE)
        for ref in sources[1:]:
            total += ref[...].astype(WIDE)
        out_ref[at, :] = total.astype(LOW)


def sum_kernel(count, *refs):
    total = refs[0][...].astype(WIDE)
    for i in range(1, count):
        total += refs[i][...].astype(WIDE)
    refs[-1][...] = total.astype(LOW)


def expert_kernel(core_ref, x_own_ref, x_far_ref, dy_own_ref, dy_far_ref, named_ref, wide_ref, *rest):
    weights, rest = rest[:24], rest[24:]
    (dense_ref, dx_own_ref, dx_far_ref, y_own_ref, y_far_ref), rest = rest[:5], rest[5:]
    grads, (x_ref, dy_ref, dx_acc, y_acc, dd_acc, split_ref) = rest[:8], rest[8:]
    step = pl.program_id(0)
    steps = pl.num_programs(0)
    early = step < steps // 2

    @pl.when(step == 0)
    def _():
        x_ref[:ROWS, :] = x_own_ref[...]
        x_ref[ROWS:, :] = x_far_ref[...]
        dy_ref[:ROWS, :] = dy_own_ref[...]
        dy_ref[ROWS:, :] = dy_far_ref[...]
        logits = dot_nt(x_ref[...], wide_ref[ROUTER_ROW : ROUTER_ROW + EXPERTS, :])
        named = named_ref[...].astype(WIDE) > 0.5
        logits = jnp.where(named, logits, NEGATIVE)
        peak = jnp.max(logits, axis=1, keepdims=True)
        expo = jnp.where(named, jnp.exp(logits - peak), 0.0)
        dense = expo / jnp.sum(expo, axis=1, keepdims=True)
        dense_ref[...] = dense
        high = dense.astype(LOW)
        split_ref[...] = jnp.concatenate([high, (dense - high.astype(WIDE)).astype(LOW)], axis=1)
        dx_acc[...] = jnp.zeros_like(dx_acc)
        y_acc[...] = jnp.zeros_like(y_acc)
        dd_acc[...] = jnp.zeros_like(dd_acc)

    x = x_ref[...]
    dy = dy_ref[...]
    gate_w, up_w, down_w = (
        jnp.concatenate(
            [
                jnp.where(early, weights[m * 8 + k * 2][0], weights[m * 8 + k * 2 + 1][0])
                for k in range(4)
            ],
            axis=1,
        )
        for m in range(3)
    )
    first = core_ref[0] * HALF_EXPERTS + step * (STEP_ROWS // UNITS)
    expert = lax.broadcasted_iota(jnp.int32, (2 * EXPERTS, STEP_ROWS), 0) % EXPERTS
    unit = lax.broadcasted_iota(jnp.int32, (2 * EXPERTS, STEP_ROWS), 1)
    spread = (expert == first + unit // UNITS).astype(WIDE).astype(LOW)
    dense = dot_nn(split_ref[...], spread)
    gate_up_w = jnp.concatenate([gate_w, up_w], axis=0)
    pre = dot_nt(x, gate_up_w)
    gate_pre, up_pre = pre[:, :STEP_ROWS], pre[:, STEP_ROWS:]
    dscaled = dot_nt(dy, down_w)
    sigmoid = 1.0 / (1.0 + jnp.exp(-gate_pre))
    silu = gate_pre * sigmoid
    active = silu * up_pre
    scaled = (active * dense).astype(LOW)
    dd_acc[...] += dot_nt((dscaled * active).astype(LOW), spread[:EXPERTS])
    dactive = dscaled * dense
    dgate = (dactive * up_pre * sigmoid * (1.0 + gate_pre * (1.0 - sigmoid))).astype(LOW)
    dup = (dactive * silu).astype(LOW)
    y_acc[...] += dot_nn(scaled, down_w)
    dgate_up = jnp.concatenate([dgate, dup], axis=1)
    dx_acc[...] += dot_nn(dgate_up, gate_up_w)
    product = dot_tn(dgate_up, x).astype(LOW)
    products = [product[:STEP_ROWS], product[STEP_ROWS:], dot_tn(scaled, dy).astype(LOW)]

    def store(half):
        for m in range(3):
            for k in range(4):
                grads[2 * k + half][m] = products[m][:, k * CHUNK : (k + 1) * CHUNK]

    pl.when(early)(functools.partial(store, 0))
    pl.when(jnp.logical_not(early))(functools.partial(store, 1))

    @pl.when(step == steps - 1)
    def _():
        fill = jnp.zeros((ROWS, 128 - EXPERTS), LOW)
        y_own_ref[...] = y_acc[:ROWS, :].astype(LOW)
        y_far_ref[...] = y_acc[ROWS:, :].astype(LOW)
        dx_own_ref[:, :WIDTH] = dx_acc[:ROWS, :].astype(LOW)
        dx_own_ref[:, WIDTH:] = jnp.concatenate([dd_acc[:ROWS, :].astype(LOW), fill], axis=1)
        dx_far_ref[:, :WIDTH] = dx_acc[ROWS:, :].astype(LOW)
        dx_far_ref[:, WIDTH:] = jnp.concatenate([dd_acc[ROWS:, :].astype(LOW), fill], axis=1)


ANY = pl.BlockSpec(memory_space=pl.ANY)
SMEM = pl.BlockSpec(memory_space=pltpu.SMEM)
WHOLE = pl.BlockSpec(memory_space=pltpu.VMEM)


def local_call(kernel, outs, *operands, after=(), scalars=(), name, us=2.0):
    skip = len(after)

    def run(*refs):
        kernel(*refs[skip:])

    return pl.pallas_call(
        run,
        in_specs=[ANY] * skip + [SMEM] * len(scalars) + [WHOLE] * len(operands),
        out_specs=[WHOLE] * len(outs),
        out_shape=[jax.ShapeDtypeStruct(shape, dtype) for shape, dtype in outs],
        compiler_params=pltpu.CompilerParams(vmem_limit_bytes=VMEM),
        cost_estimate=pl.CostEstimate(
            flops=int(us * 1e9), bytes_accessed=int(us * 3e6), transcendentals=0
        ),
        name=name,
    )(*after, *scalars, *operands)


def sum_parts(parts, after=(), name="sum_parts"):
    (total,) = local_call(
        functools.partial(sum_kernel, len(parts)), [(parts[0].shape, LOW)], *parts,
        after=after, name=name,
    )
    return total


def cut_kernel(core_ref, small_ref, table_ref, gate_ref, up_ref, down_ref, *outs):
    for half in range(2):
        for m, ref in enumerate((gate_ref, up_ref, down_ref)):
            at = half * (HALF_EXPERTS // 2)
            outs[half][m] = ref[at : at + HALF_EXPERTS // 2].reshape(HIDDEN // 2, CHUNK)


def cut_weights(core, weights, after):
    mine = pl.BlockSpec((HALF_EXPERTS, UNITS, CHUNK), lambda i, core_ref: (core_ref[0], 0, 0))
    part = (3, HIDDEN // 2, CHUNK)
    return pl.pallas_call(
        cut_kernel,
        grid_spec=pltpu.PrefetchScalarGridSpec(
            num_scalar_prefetch=1,
            grid=(1,),
            in_specs=[ANY] * 2 + [mine] * 3,
            out_specs=[pl.BlockSpec(part, lambda i, core_ref: (0, 0, 0))] * 2,
        ),
        out_shape=[jax.ShapeDtypeStruct(part, LOW)] * 2,
        compiler_params=pltpu.CompilerParams(vmem_limit_bytes=VMEM),
        name="cut_weights",
    )(core, *after, *weights)


def place_kernel(core_ref, *refs):
    sources, last_ref, (block_ref, input_ref), outs = refs[:4], refs[4], refs[5:7], refs[7:]
    input_ref[...] = last_ref[:, :WIDTH].astype(WIDE)
    block_ref[...] = last_ref[:, WIDTH:]
    whose, half = pl.program_id(0), pl.program_id(1)
    mine = whose == core_ref[0]
    for h in range(2):
        for own in range(2):

            @pl.when((half == h) & (mine == (own == 1)))
            def _():
                source = sources[2 * h + (0 if own else 1)]
                for m in range(3):
                    outs[m][...] = (
                        source[m].astype(WIDE).reshape(HALF_EXPERTS // 2, UNITS, CHUNK)
                    )


def place_grads(core, sources, last):
    return pl.pallas_call(
        place_kernel,
        grid=(2, 2),
        in_specs=[SMEM]
        + [pl.BlockSpec((3, HIDDEN // 2, CHUNK), lambda i, j: (0, 0, 0))] * 4
        + [pl.BlockSpec((ROWS // 4, 2 * WIDTH), lambda i, j: (2 * i + j, 0))],
        out_specs=[pl.BlockSpec((ROWS // 4, WIDTH), lambda i, j: (2 * i + j, 0))] * 2
        + [pl.BlockSpec((HALF_EXPERTS // 2, UNITS, CHUNK), lambda i, j: (2 * i + j, 0, 0))] * 3,
        out_shape=[
            jax.ShapeDtypeStruct((ROWS, WIDTH), LOW),
            jax.ShapeDtypeStruct((ROWS, WIDTH), WIDE),
        ]
        + [jax.ShapeDtypeStruct((EXPERTS, UNITS, CHUNK), WIDE)] * 3,
        compiler_params=pltpu.CompilerParams(vmem_limit_bytes=VMEM),
        name="place_grads",
    )(core, *sources, last)


def attend(query, kv, first, last, places, out_w, after=()):
    skip = len(after)
    shapes = [
        jax.ShapeDtypeStruct((ROWS, 128), LOW),
        jax.ShapeDtypeStruct((ROWS, WIDTH), LOW),
    ] + [
        jax.ShapeDtypeStruct((2 * BLOCK, (j + 1) * N_CTX * BLOCK), LOW) for j in range(SLOTS)
    ]

    def run(*refs):
        attend_kernel(*refs[skip:])

    return pl.pallas_call(
        run,
        in_specs=[ANY] * skip + [WHOLE] * 6,
        out_specs=[WHOLE] * len(shapes),
        out_shape=shapes,
        cost_estimate=pl.CostEstimate(flops=6 * 10**9, bytes_accessed=10**7, transcendentals=0),
        scratch_shapes=[pltpu.VMEM((N_CTX * ROWS, HEAD_DIM), LOW)] * 2,
        compiler_params=pltpu.CompilerParams(vmem_limit_bytes=VMEM),
        name="attend",
    )(*after, query, kv, first, last, places, out_w)


def attend_back(query, kv, dresid, out_w, probs, after=()):
    skip = len(after)

    def run(*refs):
        attend_back_kernel(*refs[skip:])

    return pl.pallas_call(
        run,
        in_specs=[ANY] * skip + [WHOLE] * (4 + SLOTS),
        out_specs=[WHOLE] * 2,
        cost_estimate=pl.CostEstimate(flops=6 * 10**9, bytes_accessed=10**7, transcendentals=0),
        out_shape=[
            jax.ShapeDtypeStruct((ROWS, 128), WIDE),
            jax.ShapeDtypeStruct((N_CTX * ROWS, 128), LOW),
        ],
        scratch_shapes=[pltpu.VMEM((N_CTX * ROWS, HEAD_DIM), LOW)] * 2
        + [pltpu.VMEM((N_CTX * ROWS, HEAD_DIM), WIDE)] * 2
        + [pltpu.VMEM((ROWS, 128), LOW)],
        compiler_params=pltpu.CompilerParams(vmem_limit_bytes=VMEM),
        name="attend_back",
    )(*after, query, kv, dresid, out_w, *probs)


def experts(core, x_own, x_far, dy_own, dy_far, named, wide, pieces):
    whole = lambda shape: pl.BlockSpec(shape, lambda i: (0,) * len(shape))
    rows = 2 * ROWS
    half_steps = HIDDEN // STEP_ROWS // 2
    weight_specs = [
        pl.BlockSpec((1, STEP_ROWS, CHUNK), functools.partial(index, m))
        for m in range(3)
        for _ in range(4)
        for index in (
            lambda m, i: (m, jnp.minimum(i, half_steps - 1), 0),
            lambda m, i: (m, jnp.maximum(i - half_steps, 0), 0),
        )
    ]
    grad_specs = [
        pl.BlockSpec((3, STEP_ROWS, CHUNK), lambda i: (0, jnp.minimum(i, half_steps - 1), 0)),
        pl.BlockSpec((3, STEP_ROWS, CHUNK), lambda i: (0, jnp.maximum(i - half_steps, 0), 0)),
    ]
    return pl.pallas_call(
        expert_kernel,
        grid=(HIDDEN // STEP_ROWS,),
        in_specs=[SMEM]
        + [whole((ROWS, WIDTH))] * 4
        + [whole((rows, EXPERTS)), whole(wide.shape)]
        + weight_specs,
        out_specs=[
            whole((rows, EXPERTS)),
            whole((ROWS, WIDTH + 128)),
            whole((ROWS, WIDTH + 128)),
            whole((ROWS, WIDTH)),
            whole((ROWS, WIDTH)),
        ]
        + grad_specs * 4,
        out_shape=[
            jax.ShapeDtypeStruct((rows, EXPERTS), WIDE),
            jax.ShapeDtypeStruct((ROWS, WIDTH + 128), LOW),
            jax.ShapeDtypeStruct((ROWS, WIDTH + 128), LOW),
            jax.ShapeDtypeStruct((ROWS, WIDTH), LOW),
            jax.ShapeDtypeStruct((ROWS, WIDTH), LOW),
        ]
        + [jax.ShapeDtypeStruct((3, HIDDEN // 2, CHUNK), LOW)] * 8,
        scratch_shapes=[
            pltpu.VMEM((rows, WIDTH), LOW),
            pltpu.VMEM((rows, WIDTH), LOW),
            pltpu.VMEM((rows, WIDTH), WIDE),
            pltpu.VMEM((rows, WIDTH), WIDE),
            pltpu.VMEM((rows, EXPERTS), WIDE),
            pltpu.VMEM((rows, 2 * EXPERTS), LOW),
        ],
        compiler_params=pltpu.CompilerParams(
            vmem_limit_bytes=VMEM, dimension_semantics=("arbitrary",)
        ),
        cost_estimate=pl.CostEstimate(
            flops=25 * 10**9, bytes_accessed=3 * 10**7, transcendentals=0
        ),
        name="experts",
    )(
        core, x_own, x_far, dy_own, dy_far, named, wide,
        *[pieces[k][half] for _ in range(3) for k in range(4) for half in range(2)],
    )


def body(
    inputs,
    cotangent,
    routes,
    seq_lengths,
    block_order,
    attn_gain,
    query_weight,
    key_weight,
    value_weight,
    output_weight,
    ffn_gain,
    router_weight,
    gate_weight,
    up_weight,
    down_weight,
):
    dp = lax.axis_index("dp")
    ctx = lax.axis_index("ctx")
    tp = lax.axis_index("tp")
    core = ctx % 2

    core_at = core.reshape(1).astype(jnp.int32)
    tp_at = tp.reshape(1).astype(jnp.int32)
    dp_at = dp.reshape(1).astype(jnp.int32)

    small = jnp.concatenate(
        [
            query_weight.T,
            key_weight.T,
            value_weight.T,
            output_weight.T,
            router_weight.T,
            attn_gain[None],
            ffn_gain[None],
            jnp.zeros((14, CHUNK), LOW),
        ],
        axis=0,
    )
    small_parts = [small] + [from_dp(small, k) for k in (1, 2, 3)]

    rows_low = turn(inputs, dp * CHUNK)
    grad_low = turn(cotangent, dp * CHUNK)
    named = jnp.sum(
        (routes[:, :, None] == jnp.arange(EXPERTS, dtype=jnp.int32)[None, None, :]).astype(WIDE),
        axis=1,
    ).astype(LOW)
    grad_far = swap_ctx(grad_low, 1)
    named_both = jnp.concatenate([named, swap_ctx(named, 1)], axis=0)

    order = block_order[0]
    offsets = jnp.arange(BLOCK, dtype=jnp.int32)
    mine = lax.dynamic_slice_in_dim(order, ctx * SLOTS, SLOTS)
    my_places = (mine[:, None] * BLOCK + offsets[None, :]).reshape(ROWS, 1)
    lengths = seq_lengths[0]
    ends = jnp.cumsum(lengths)
    passed = (my_places >= ends[None, :]).astype(jnp.int32)
    my_first = jnp.sum(passed * lengths[None, :], axis=1, keepdims=True)
    inner = (my_places - my_first).astype(WIDE)
    by_slot = order.reshape(N_CTX, SLOTS).T.reshape(-1)
    key_places = (by_slot[:, None] * BLOCK + offsets[None, :]).reshape(1, N_CTX * ROWS)
    half = HEAD_DIM // 2
    freqs = 10000.0 ** (-jnp.arange(half, dtype=WIDE) / half)
    angle = inner * freqs[None, :]
    cosine = jnp.cos(angle)
    sine = jnp.sin(angle)
    cos_six = jnp.concatenate([cosine] * 6, axis=1)
    sin_six = jnp.concatenate([-sine, sine] * 3, axis=1)

    own = cut_weights(core_at, (gate_weight, up_weight, down_weight), (small, sin_six))
    right = [from_dp(part, 1) for part in own]
    left = [from_dp(part, 3) for part in own]
    across = [from_dp(right[0], 1), from_dp(left[1], 3)]
    pieces = [own, right, across, left]

    wide, out_w, normed, query, kv = local_call(
        project_kernel,
        [
            ((PACK_ROWS, WIDTH), LOW),
            ((128, WIDTH), LOW),
            ((ROWS, WIDTH), LOW),
            ((ROWS, 128), LOW),
            ((ROWS, 128), LOW),
        ],
        rows_low, *small_parts, cos_six, sin_six,
        name="project",
    )
    kv_all = lax.all_gather(kv, "ctx", axis=0, tiled=True)
    attended, attn_part, *probs = attend(
        query, kv_all, my_first, my_places, key_places, out_w, after=(right[0], left[0])
    )

    attn_parts = lax.all_to_all(attn_part, "tp", 0, 0, tiled=True).reshape(N_TP, PART, WIDTH)
    resid, normed_sent = local_call(
        norm_kernel,
        [((PART, WIDTH), WIDE), ((ROWS, WIDTH), LOW)],
        attn_parts, rows_low, wide,
        scalars=(tp_at,), after=(right[1], left[1]), name="norm",
    )
    normed_two = lax.all_to_all(normed_sent, "tp", 0, 0, tiled=True)
    normed_far = swap_ctx(normed_two, 1)

    dense, dx_own, dx_far, y_own, y_far, *grads = experts(
        core_at, normed_two, normed_far, grad_low, grad_far, named_both, wide, pieces
    )
    chunks = [grads[2 * k : 2 * k + 2] for k in range(4)]

    by_left = to_dp(chunks[2][0], 1)
    by_right = to_dp(chunks[2][1], 3)
    straight = [to_dp(chunks[3][0], 3), to_dp(chunks[1][1], 1)]

    dx = (dx_own.astype(WIDE) + swap_ctx(dx_far, 1).astype(WIDE)).astype(LOW)
    dx_parts = lax.all_to_all(dx, "tp", 0, 0, tiled=True).reshape(N_TP, PART, WIDTH + 128)
    relay_right = sum_parts([chunks[1][0], by_left])
    relay_left = sum_parts([chunks[3][1], by_right])
    dresid, gain_two_part, sent = local_call(
        norm_back_kernel,
        [((PART, WIDTH), WIDE), ((1, WIDTH), WIDE), ((ROWS, WIDTH + 128), LOW)],
        dx_parts, resid, dense, grad_low, wide,
        scalars=(tp_at,), after=(relay_right, relay_left), name="norm_back",
    )
    relayed = [to_dp(relay_right, 1), to_dp(relay_left, 3)]
    first, second = ([chunks[0][h], straight[h], relayed[h]] for h in range(2))
    back = lax.all_to_all(sent, "tp", 0, 0, tiled=True)
    dlogits_low = back[:, WIDTH : WIDTH + EXPERTS]
    first_half = sum_parts(first)
    first_other = swap_ctx(first_half, 2)
    dq, dkv = attend_back(query, kv_all, back, out_w, probs, after=(first_half,))
    y = sum_parts([y_own, swap_ctx(y_far, 1)], after=(dq, first_other))
    y_parts = lax.all_to_all(y, "tp", 0, 0, tiled=True).reshape(N_TP, PART, WIDTH)
    second_half = sum_parts(second, after=(y,))
    second_other = swap_ctx(second_half, 2)
    dkv_parts = lax.all_to_all(dkv, "ctx", 0, 0, tiled=True).reshape(N_CTX, ROWS, 128)
    dnorm_one, *small_chunks = local_call(
        project_back_kernel,
        [((ROWS, WIDTH + 128), LOW)] + [((GAIN_ROW, CHUNK), LOW)] * N_DP,
        dq, dkv_parts, cos_six, sin_six, normed, rows_low, wide,
        dot_tn(attended, back[:, :WIDTH]).astype(LOW),
        dot_tn(dlogits_low, normed_two).astype(LOW),
        gain_two_part,
        after=(second_half,),
        name="project_back", us=4.0,
    )

    dnorm_parts = lax.all_to_all(dnorm_one, "tp", 0, 0, tiled=True).reshape(
        N_TP, PART, WIDTH + 128
    )
    small_parts = [small_chunks[0]] + [to_dp(small_chunks[k], k) for k in (1, 2, 3)]
    sent, *gain_chunks = local_call(
        last_kernel,
        [((ROWS, 2 * WIDTH), LOW)] + [((16, CHUNK), LOW)] * N_DP,
        dnorm_parts, dresid, rows_low, wide, y_parts, resid,
        scalars=(jnp.concatenate([tp_at, dp_at]),), after=tuple(small_parts[1:]),
        name="last",
    )
    last = lax.all_to_all(sent, "tp", 0, 0, tiled=True)
    gain_parts = [gain_chunks[0]] + [to_dp(gain_chunks[k], k) for k in (1, 2, 3)]
    (small_sum,) = local_call(
        small_kernel, [((PACK_ROWS, CHUNK), LOW)], *small_parts, *gain_parts,
        after=(second_other,), name="small"
    )
    small_sum = sum_parts([small_sum, swap_ctx(small_sum, 1)])
    small_sum = small_sum.astype(WIDE) + swap_ctx(small_sum, 2).astype(WIDE)

    first_half = sum_parts([first_half, first_other], after=(sent,))
    second_half = sum_parts([second_half, second_other], after=(last,))
    block_output, input_grad, *expert_grads = place_grads(
        core_at,
        [first_half, swap_ctx(first_half, 1), second_half, swap_ctx(second_half, 1)],
        last,
    )
    return (
        block_output,
        input_grad,
        small_sum[GAIN_ROW],
        small_sum[:128].T,
        small_sum[128:192].T,
        small_sum[192:256].T,
        small_sum[256:384].T,
        small_sum[GAIN_ROW + 1],
        small_sum[384:416].T,
        *expert_grads,
    )


def solution(mesh):
    placed = (
        P(("dp", "ctx"), None),
        P(("dp", "ctx"), None),
        P(("dp", "ctx"), None),
        P("dp", None),
        P("dp", None),
        P("dp"),
        P("dp", "tp"),
        P("dp", "tp"),
        P("dp", "tp"),
        P("dp", "tp"),
        P("dp"),
        P("dp", None),
        P(None, "tp", "dp"),
        P(None, "tp", "dp"),
        P(None, "tp", "dp"),
    )
    return jax.shard_map(
        body,
        mesh=mesh,
        in_specs=placed,
        out_specs=(
            P(("dp", "ctx"), None),
            P(("dp", "ctx"), None),
            P("dp"),
            P("dp", "tp"),
            P("dp", "tp"),
            P("dp", "tp"),
            P("dp", "tp"),
            P("dp"),
            P("dp", None),
            P(None, "tp", "dp"),
            P(None, "tp", "dp"),
            P(None, "tp", "dp"),
        ),
        check_vma=False,
    )
```

```python
import functools

import jax
import jax.numpy as jnp
from jax import lax
from jax.experimental import pallas as pl
from jax.experimental.pallas import tpu as pltpu
from jax.sharding import PartitionSpec as P

HEADS = 16
KV_HEADS = 8
HEAD_DIM = 64
BLOCK = 64
ROWS = 384
WIDTH = 1024
CHUNK = 256
SLOTS = 6
N_CTX = 4
N_DP = 4
N_TP = 8
PART = ROWS // N_TP
EXPERTS = 32
HALF_EXPERTS = 16
UNITS = 64
HIDDEN = HALF_EXPERTS * UNITS
STEP_ROWS = 256
QKV_ROWS = 256
ROPED = 192
ROUTER_ROW = 384
GAIN_ROW = 416
PACK_ROWS = 432
VMEM = 56 * 1024 * 1024

EPSILON = 1e-05
NEGATIVE = -1e30
SCALE = HEAD_DIM**-0.5
LOW = jnp.bfloat16
WIDE = jnp.float32


def dot_nn(left, right):
    return lax.dot_general(left, right, (((1,), (0,)), ((), ())), preferred_element_type=WIDE)


def dot_nt(left, right):
    return lax.dot_general(left, right, (((1,), (1,)), ((), ())), preferred_element_type=WIDE)


def dot_tn(left, right):
    return lax.dot_general(left, right, (((0,), (0,)), ((), ())), preferred_element_type=WIDE)


def turn(values, start):
    return lax.dynamic_slice_in_dim(
        jnp.concatenate([values, values], axis=1), start, values.shape[1], axis=1
    )


def from_dp(values, k):
    return lax.ppermute(values, "dp", [(s, (s - k) % N_DP) for s in range(N_DP)])


def to_dp(values, k):
    return lax.ppermute(values, "dp", [(s, (s + k) % N_DP) for s in range(N_DP)])


def swap_ctx(values, bit):
    return lax.ppermute(values, "ctx", [(s, s ^ bit) for s in range(N_CTX)])


def split_heads(values):
    return jnp.concatenate([values[:, :HEAD_DIM], values[:, HEAD_DIM:]], axis=0)


def join_heads(values):
    return jnp.concatenate([values[:BLOCK], values[BLOCK:]], axis=1)


def attend_kernel(q_ref, kv_ref, first_ref, last_ref, place_ref, out_w_ref, att_ref, sum_ref, *rest):
    probs_refs, (k_ref, v_ref) = rest[:SLOTS], rest[SLOTS:]
    for j in range(SLOTS):
        for c in range(N_CTX):
            rows = kv_ref[c * ROWS + j * BLOCK : c * ROWS + (j + 1) * BLOCK, :]
            at = (j * N_CTX + c) * BLOCK
            k_ref[at : at + BLOCK, :] = rows[:, :HEAD_DIM]
            v_ref[at : at + BLOCK, :] = rows[:, HEAD_DIM:]
    for j in range(SLOTS):
        rows = slice(j * BLOCK, (j + 1) * BLOCK)
        keys = (j + 1) * N_CTX * BLOCK
        query = split_heads(q_ref[rows, :])
        scores = dot_nt(query, k_ref[:keys, :]) * SCALE
        places = place_ref[:, :keys]
        kept = (places >= first_ref[rows, :]) & (places <= last_ref[rows, :])
        kept = jnp.concatenate([kept, kept], axis=0)
        scores = jnp.where(kept, scores, NEGATIVE)
        peak = jnp.max(scores, axis=1, keepdims=True)
        expo = jnp.exp(scores - peak)
        total = jnp.sum(expo, axis=1, keepdims=True)
        probs = (expo * (1.0 / total)).astype(LOW)
        probs_refs[j][...] = probs
        mixed = dot_nn(probs, v_ref[:keys, :]).astype(LOW)
        att_ref[rows, :] = join_heads(mixed)
    sum_ref[...] = dot_nn(att_ref[...], out_w_ref[...]).astype(LOW)


def attend_back_kernel(q_ref, kv_ref, dres_ref, out_w_ref, *rest):
    probs_refs = rest[:SLOTS]
    dq_ref, dkv_ref, k_ref, v_ref, dk_ref, dv_ref, datt_ref = rest[SLOTS:]
    datt_ref[...] = dot_nt(dres_ref[:, :WIDTH], out_w_ref[...]).astype(LOW)
    for j in range(SLOTS):
        for c in range(N_CTX):
            rows = kv_ref[c * ROWS + j * BLOCK : c * ROWS + (j + 1) * BLOCK, :]
            at = (j * N_CTX + c) * BLOCK
            k_ref[at : at + BLOCK, :] = rows[:, :HEAD_DIM]
            v_ref[at : at + BLOCK, :] = rows[:, HEAD_DIM:]
    for j in reversed(range(SLOTS)):
        rows = slice(j * BLOCK, (j + 1) * BLOCK)
        keys = (j + 1) * N_CTX * BLOCK
        query = split_heads(q_ref[rows, :])
        dmix = split_heads(datt_ref[rows, :])
        probs = probs_refs[j][...]
        wide = probs.astype(WIDE)
        dprobs = dot_nt(dmix, v_ref[:keys, :])
        delta = jnp.sum(wide * dprobs, axis=1, keepdims=True)
        dscores = (wide * (dprobs - delta)).astype(LOW)
        dq_ref[rows, :] = join_heads(dot_nn(dscores, k_ref[:keys, :]) * SCALE)
        dk = dot_tn(dscores, query) * SCALE
        dv = dot_tn(probs, dmix)
        if j == SLOTS - 1:
            dk_ref[...] = dk
            dv_ref[...] = dv
        else:
            dk_ref[:keys, :] += dk
            dv_ref[:keys, :] += dv
    for j in range(SLOTS):
        for c in range(N_CTX):
            at = (j * N_CTX + c) * BLOCK
            dkv_ref[c * ROWS + j * BLOCK : c * ROWS + (j + 1) * BLOCK, :] = jnp.concatenate(
                [dk_ref[at : at + BLOCK, :], dv_ref[at : at + BLOCK, :]], axis=1
            ).astype(LOW)


def swap_halves(values):
    half = HEAD_DIM // 2
    parts = []
    for at in range(0, values.shape[1], HEAD_DIM):
        parts += [values[:, at + half : at + HEAD_DIM], values[:, at : at + half]]
    return jnp.concatenate(parts, axis=1)


def project_kernel(x_ref, *rest):
    parts, (cos_ref, sin_ref), outs = rest[:N_DP], rest[N_DP : N_DP + 2], rest[N_DP + 2 :]
    wide_ref, out_w_ref, normed_ref, q_ref, kv_ref = outs
    for k in range(N_DP):
        wide_ref[:, k * CHUNK : (k + 1) * CHUNK] = parts[k][...]
    out_w_ref[...] = wide_ref[QKV_ROWS:ROUTER_ROW, :]
    x = x_ref[...].astype(WIDE)
    inverse = lax.rsqrt(jnp.mean(x * x, axis=1, keepdims=True) + EPSILON)
    gain = wide_ref[GAIN_ROW : GAIN_ROW + 16, :].astype(WIDE)[:1]
    normed = (x * inverse * gain).astype(LOW)
    normed_ref[...] = normed
    lin = dot_nt(normed, wide_ref[:QKV_ROWS, :])
    turned = lin[:, :ROPED] * cos_ref[...] + swap_halves(lin[:, :ROPED]) * sin_ref[...]
    q_ref[...] = turned[:, :128].astype(LOW)
    kv_ref[...] = jnp.concatenate([turned[:, 128:], lin[:, ROPED:]], axis=1).astype(LOW)


def norm_kernel(tp_ref, parts_ref, x_ref, wide_ref, resid_ref, normed_ref):
    at = pl.ds(pl.multiple_of(tp_ref[0] * PART, PART), PART)
    resid = x_ref[at, :].astype(WIDE)
    total = parts_ref[0].astype(WIDE)
    for i in range(1, N_TP):
        total += parts_ref[i].astype(WIDE)
    resid = resid + total
    resid_ref[...] = resid
    gain = wide_ref[GAIN_ROW : GAIN_ROW + 16, :].astype(WIDE)[1:2]
    inverse = lax.rsqrt(jnp.mean(resid * resid, axis=1, keepdims=True) + EPSILON)
    normed = (resid * inverse * gain).astype(LOW)
    for i in range(N_TP):
        normed_ref[i * PART : (i + 1) * PART, :] = normed


def norm_back_kernel(
    tp_ref, parts_ref, resid_ref, dense_ref, dy_ref, wide_ref, dresid_ref, gain_ref, sent_ref
):
    at = pl.ds(pl.multiple_of(tp_ref[0] * PART, PART), PART)
    total = parts_ref[0].astype(WIDE)
    for i in range(1, N_TP):
        total += parts_ref[i].astype(WIDE)
    dense = dense_ref[at, :]
    ddense = total[:, WIDTH : WIDTH + EXPERTS]
    dlogits = dense * (ddense - jnp.sum(dense * ddense, axis=1, keepdims=True))
    dlow = dlogits.astype(LOW)
    drest = (dlogits - dlow.astype(WIDE)).astype(LOW)
    router = wide_ref[ROUTER_ROW : ROUTER_ROW + EXPERTS, :]
    dnorm = total[:, :WIDTH] + dot_nn(dlow, router) + dot_nn(drest, router)
    resid = resid_ref[...]
    inverse = lax.rsqrt(jnp.mean(resid * resid, axis=1, keepdims=True) + EPSILON)
    gain = wide_ref[GAIN_ROW : GAIN_ROW + 16, :].astype(WIDE)[1:2]
    gain_ref[...] = jnp.sum(dnorm * resid * inverse, axis=0, keepdims=True)
    weighted = dnorm * gain
    dresid = (
        dy_ref[at, :].astype(WIDE)
        + inverse * weighted
        - resid * inverse**3 * jnp.mean(weighted * resid, axis=1, keepdims=True)
    )
    dresid_ref[...] = dresid
    sent = jnp.concatenate(
        [dresid.astype(LOW), dlow, jnp.zeros((PART, 128 - EXPERTS), LOW)], axis=1
    )
    for i in range(N_TP):
        sent_ref[i * PART : (i + 1) * PART, :] = sent


def project_back_kernel(
    dq_ref, dkv_ref, cos_ref, sin_ref, normed_ref, x_ref, wide_ref, go_ref, gr_ref, gain_ref,
    dnorm_ref, *chunks
):
    dkv = dkv_ref[0].astype(WIDE)
    for i in range(1, N_CTX):
        dkv += dkv_ref[i].astype(WIDE)
    turned = jnp.concatenate([dq_ref[...], dkv[:, :HEAD_DIM]], axis=1)
    turned = turned * cos_ref[...] - swap_halves(turned) * sin_ref[...]
    dlin = jnp.concatenate([turned, dkv[:, HEAD_DIM:]], axis=1).astype(LOW)
    dnorm = dot_nn(dlin, wide_ref[:QKV_ROWS, :])
    dnorm_ref[:, :WIDTH] = dnorm.astype(LOW)
    x = x_ref[...].astype(WIDE)
    inverse = lax.rsqrt(jnp.mean(x * x, axis=1, keepdims=True) + EPSILON)
    gain_one = jnp.sum(dnorm * (x * inverse), axis=0, keepdims=True)
    extra = [
        part[:, i * 128 : (i + 1) * 128] for part in (gain_one, gain_ref[...]) for i in range(8)
    ]
    extra = jnp.concatenate([*extra, jnp.zeros((PART - 16, 128), WIDE)], axis=0).astype(LOW)
    for i in range(N_TP):
        dnorm_ref[i * PART : (i + 1) * PART, WIDTH:] = extra
    product = dot_tn(dlin, normed_ref[...]).astype(LOW)
    for k in range(N_DP):
        at = slice(k * CHUNK, (k + 1) * CHUNK)
        chunks[k][:QKV_ROWS, :] = product[:, at]
        chunks[k][QKV_ROWS:ROUTER_ROW, :] = go_ref[:, at]
        chunks[k][ROUTER_ROW:GAIN_ROW, :] = gr_ref[:, at]


def last_kernel(at_ref, parts_ref, dresid_ref, x_ref, wide_ref, y_ref, resid_ref, sent_ref, *gains):
    at = pl.ds(pl.multiple_of(at_ref[0] * PART, PART), PART)
    total = parts_ref[0].astype(WIDE)
    for i in range(1, N_TP):
        total += parts_ref[i].astype(WIDE)
    dnorm = total[:, :WIDTH]
    for k in range(N_DP):
        rows = [
            jnp.concatenate([total[r : r + 1, WIDTH:] for r in (2 * k + g, 2 * k + g + 1)], axis=1)
            for g in (0, 8)
        ]
        gains[k][...] = jnp.concatenate([*rows, jnp.zeros((14, CHUNK), WIDE)], axis=0).astype(LOW)
    x = x_ref[at, :].astype(WIDE)
    inverse = lax.rsqrt(jnp.mean(x * x, axis=1, keepdims=True) + EPSILON)
    gain = wide_ref[GAIN_ROW : GAIN_ROW + 16, :].astype(WIDE)[:1]
    weighted = dnorm * gain
    dx = (
        dresid_ref[...]
        + inverse * weighted
        - x * inverse**3 * jnp.mean(weighted * x, axis=1, keepdims=True)
    )
    out = resid_ref[...]
    for i in range(N_TP):
        out += y_ref[i].astype(WIDE)
    home = at_ref[1] * CHUNK
    sent = [pltpu.roll(v, home, 1).astype(LOW) for v in (dx, out)]
    for i in range(N_TP):
        sent_ref[i * PART : (i + 1) * PART, :WIDTH] = sent[0]
        sent_ref[i * PART : (i + 1) * PART, WIDTH:] = sent[1]


def small_kernel(*refs):
    parts, gains, out_ref = refs[:N_DP], refs[N_DP : 2 * N_DP], refs[-1]
    for sources, at in ((parts, slice(0, GAIN_ROW)), (gains, slice(GAIN_ROW, PACK_ROWS))):
        total = sources[0][...].astype(WIDE)
        for ref in sources[1:]:
            total += ref[...].astype(WIDE)
        out_ref[at, :] = total.astype(LOW)


def sum_kernel(count, *refs):
    total = refs[0][...].astype(WIDE)
    for i in range(1, count):
        total += refs[i][...].astype(WIDE)
    refs[-1][...] = total.astype(LOW)


def expert_kernel(core_ref, x_own_ref, x_far_ref, dy_own_ref, dy_far_ref, named_ref, wide_ref, *rest):
    weights, rest = rest[:24], rest[24:]
    (dense_ref, dx_own_ref, dx_far_ref, y_own_ref, y_far_ref), rest = rest[:5], rest[5:]
    grads, (x_ref, dy_ref, dx_acc, y_acc, dd_acc, split_ref) = rest[:8], rest[8:]
    step = pl.program_id(0)
    steps = pl.num_programs(0)
    early = step < steps // 2

    @pl.when(step == 0)
    def _():
        x_ref[:ROWS, :] = x_own_ref[...]
        x_ref[ROWS:, :] = x_far_ref[...]
        dy_ref[:ROWS, :] = dy_own_ref[...]
        dy_ref[ROWS:, :] = dy_far_ref[...]
        logits = dot_nt(x_ref[...], wide_ref[ROUTER_ROW : ROUTER_ROW + EXPERTS, :])
        named = named_ref[...].astype(WIDE) > 0.5
        logits = jnp.where(named, logits, NEGATIVE)
        peak = jnp.max(logits, axis=1, keepdims=True)
        expo = jnp.where(named, jnp.exp(logits - peak), 0.0)
        dense = expo / jnp.sum(expo, axis=1, keepdims=True)
        dense_ref[...] = dense
        high = dense.astype(LOW)
        split_ref[...] = jnp.concatenate([high, (dense - high.astype(WIDE)).astype(LOW)], axis=1)
        dx_acc[...] = jnp.zeros_like(dx_acc)
        y_acc[...] = jnp.zeros_like(y_acc)
        dd_acc[...] = jnp.zeros_like(dd_acc)

    x = x_ref[...]
    dy = dy_ref[...]
    gate_w, up_w, down_w = (
        jnp.concatenate(
            [
                jnp.where(early, weights[m * 8 + k * 2][0], weights[m * 8 + k * 2 + 1][0])
                for k in range(4)
            ],
            axis=1,
        )
        for m in range(3)
    )
    first = core_ref[0] * HALF_EXPERTS + step * (STEP_ROWS // UNITS)
    expert = lax.broadcasted_iota(jnp.int32, (2 * EXPERTS, STEP_ROWS), 0) % EXPERTS
    unit = lax.broadcasted_iota(jnp.int32, (2 * EXPERTS, STEP_ROWS), 1)
    spread = (expert == first + unit // UNITS).astype(WIDE).astype(LOW)
    dense = dot_nn(split_ref[...], spread)
    gate_up_w = jnp.concatenate([gate_w, up_w], axis=0)
    pre = dot_nt(x, gate_up_w)
    gate_pre, up_pre = pre[:, :STEP_ROWS], pre[:, STEP_ROWS:]
    dscaled = dot_nt(dy, down_w)
    sigmoid = 1.0 / (1.0 + jnp.exp(-gate_pre))
    silu = gate_pre * sigmoid
    active = silu * up_pre
    scaled = (active * dense).astype(LOW)
    dd_acc[...] += dot_nt((dscaled * active).astype(LOW), spread[:EXPERTS])
    dactive = dscaled * dense
    dgate = (dactive * up_pre * sigmoid * (1.0 + gate_pre * (1.0 - sigmoid))).astype(LOW)
    dup = (dactive * silu).astype(LOW)
    y_acc[...] += dot_nn(scaled, down_w)
    dgate_up = jnp.concatenate([dgate, dup], axis=1)
    dx_acc[...] += dot_nn(dgate_up, gate_up_w)
    product = dot_tn(dgate_up, x).astype(LOW)
    products = [product[:STEP_ROWS], product[STEP_ROWS:], dot_tn(scaled, dy).astype(LOW)]

    def store(half):
        for m in range(3):
            for k in range(4):
                grads[2 * k + half][m] = products[m][:, k * CHUNK : (k + 1) * CHUNK]

    pl.when(early)(functools.partial(store, 0))
    pl.when(jnp.logical_not(early))(functools.partial(store, 1))

    @pl.when(step == steps - 1)
    def _():
        fill = jnp.zeros((ROWS, 128 - EXPERTS), LOW)
        y_own_ref[...] = y_acc[:ROWS, :].astype(LOW)
        y_far_ref[...] = y_acc[ROWS:, :].astype(LOW)
        dx_own_ref[:, :WIDTH] = dx_acc[:ROWS, :].astype(LOW)
        dx_own_ref[:, WIDTH:] = jnp.concatenate([dd_acc[:ROWS, :].astype(LOW), fill], axis=1)
        dx_far_ref[:, :WIDTH] = dx_acc[ROWS:, :].astype(LOW)
        dx_far_ref[:, WIDTH:] = jnp.concatenate([dd_acc[ROWS:, :].astype(LOW), fill], axis=1)


ANY = pl.BlockSpec(memory_space=pl.ANY)
SMEM = pl.BlockSpec(memory_space=pltpu.SMEM)
WHOLE = pl.BlockSpec(memory_space=pltpu.VMEM)


def local_call(kernel, outs, *operands, after=(), scalars=(), name, us=2.0):
    skip = len(after)

    def run(*refs):
        kernel(*refs[skip:])

    return pl.pallas_call(
        run,
        in_specs=[ANY] * skip + [SMEM] * len(scalars) + [WHOLE] * len(operands),
        out_specs=[WHOLE] * len(outs),
        out_shape=[jax.ShapeDtypeStruct(shape, dtype) for shape, dtype in outs],
        compiler_params=pltpu.CompilerParams(vmem_limit_bytes=VMEM),
        cost_estimate=pl.CostEstimate(
            flops=int(us * 1e9), bytes_accessed=int(us * 3e6), transcendentals=0
        ),
        name=name,
    )(*after, *scalars, *operands)


def sum_parts(parts, after=(), name="sum_parts"):
    (total,) = local_call(
        functools.partial(sum_kernel, len(parts)), [(parts[0].shape, LOW)], *parts,
        after=after, name=name,
    )
    return total


def cut_kernel(core_ref, one_ref, two_ref, three_ref, gate_ref, up_ref, down_ref, *outs):
    for half in range(2):
        for m, ref in enumerate((gate_ref, up_ref, down_ref)):
            at = half * (HALF_EXPERTS // 2)
            outs[half][m] = ref[at : at + HALF_EXPERTS // 2].reshape(HIDDEN // 2, CHUNK)


def cut_weights(core, weights, after):
    mine = pl.BlockSpec((HALF_EXPERTS, UNITS, CHUNK), lambda i, core_ref: (core_ref[0], 0, 0))
    part = (3, HIDDEN // 2, CHUNK)
    return pl.pallas_call(
        cut_kernel,
        grid_spec=pltpu.PrefetchScalarGridSpec(
            num_scalar_prefetch=1,
            grid=(1,),
            in_specs=[ANY] * 3 + [mine] * 3,
            out_specs=[pl.BlockSpec(part, lambda i, core_ref: (0, 0, 0))] * 2,
        ),
        out_shape=[jax.ShapeDtypeStruct(part, LOW)] * 2,
        compiler_params=pltpu.CompilerParams(vmem_limit_bytes=VMEM),
        name="cut_weights",
    )(core, *after, *weights)


def place_kernel(core_ref, *refs):
    sources, last_ref, (block_ref, input_ref), outs = refs[:4], refs[4], refs[5:7], refs[7:]
    input_ref[...] = last_ref[:, :WIDTH].astype(WIDE)
    block_ref[...] = last_ref[:, WIDTH:]
    whose, half = pl.program_id(0), pl.program_id(1)
    mine = whose == core_ref[0]
    for h in range(2):
        for own in range(2):

            @pl.when((half == h) & (mine == (own == 1)))
            def _():
                source = sources[2 * h + (0 if own else 1)]
                for m in range(3):
                    outs[m][...] = (
                        source[m].astype(WIDE).reshape(HALF_EXPERTS // 2, UNITS, CHUNK)
                    )


def place_grads(core, sources, last):
    return pl.pallas_call(
        place_kernel,
        grid=(2, 2),
        in_specs=[SMEM]
        + [pl.BlockSpec((3, HIDDEN // 2, CHUNK), lambda i, j: (0, 0, 0))] * 4
        + [pl.BlockSpec((ROWS // 4, 2 * WIDTH), lambda i, j: (2 * i + j, 0))],
        out_specs=[pl.BlockSpec((ROWS // 4, WIDTH), lambda i, j: (2 * i + j, 0))] * 2
        + [pl.BlockSpec((HALF_EXPERTS // 2, UNITS, CHUNK), lambda i, j: (2 * i + j, 0, 0))] * 3,
        out_shape=[
            jax.ShapeDtypeStruct((ROWS, WIDTH), LOW),
            jax.ShapeDtypeStruct((ROWS, WIDTH), WIDE),
        ]
        + [jax.ShapeDtypeStruct((EXPERTS, UNITS, CHUNK), WIDE)] * 3,
        compiler_params=pltpu.CompilerParams(vmem_limit_bytes=VMEM),
        name="place_grads",
    )(core, *sources, last)


def attend(query, kv, first, last, places, out_w, after=()):
    skip = len(after)
    shapes = [
        jax.ShapeDtypeStruct((ROWS, 128), LOW),
        jax.ShapeDtypeStruct((ROWS, WIDTH), LOW),
    ] + [
        jax.ShapeDtypeStruct((2 * BLOCK, (j + 1) * N_CTX * BLOCK), LOW) for j in range(SLOTS)
    ]

    def run(*refs):
        attend_kernel(*refs[skip:])

    return pl.pallas_call(
        run,
        in_specs=[ANY] * skip + [WHOLE] * 6,
        out_specs=[WHOLE] * len(shapes),
        out_shape=shapes,
        cost_estimate=pl.CostEstimate(flops=6 * 10**9, bytes_accessed=10**7, transcendentals=0),
        scratch_shapes=[pltpu.VMEM((N_CTX * ROWS, HEAD_DIM), LOW)] * 2,
        compiler_params=pltpu.CompilerParams(vmem_limit_bytes=VMEM),
        name="attend",
    )(*after, query, kv, first, last, places, out_w)


def attend_back(query, kv, dresid, out_w, probs, after=()):
    skip = len(after)

    def run(*refs):
        attend_back_kernel(*refs[skip:])

    return pl.pallas_call(
        run,
        in_specs=[ANY] * skip + [WHOLE] * (4 + SLOTS),
        out_specs=[WHOLE] * 2,
        cost_estimate=pl.CostEstimate(flops=6 * 10**9, bytes_accessed=10**7, transcendentals=0),
        out_shape=[
            jax.ShapeDtypeStruct((ROWS, 128), WIDE),
            jax.ShapeDtypeStruct((N_CTX * ROWS, 128), LOW),
        ],
        scratch_shapes=[pltpu.VMEM((N_CTX * ROWS, HEAD_DIM), LOW)] * 2
        + [pltpu.VMEM((N_CTX * ROWS, HEAD_DIM), WIDE)] * 2
        + [pltpu.VMEM((ROWS, 128), LOW)],
        compiler_params=pltpu.CompilerParams(vmem_limit_bytes=VMEM),
        name="attend_back",
    )(*after, query, kv, dresid, out_w, *probs)


def experts(core, x_own, x_far, dy_own, dy_far, named, wide, pieces):
    whole = lambda shape: pl.BlockSpec(shape, lambda i: (0,) * len(shape))
    rows = 2 * ROWS
    half_steps = HIDDEN // STEP_ROWS // 2
    weight_specs = [
        pl.BlockSpec((1, STEP_ROWS, CHUNK), functools.partial(index, m))
        for m in range(3)
        for _ in range(4)
        for index in (
            lambda m, i: (m, jnp.minimum(i, half_steps - 1), 0),
            lambda m, i: (m, jnp.maximum(i - half_steps, 0), 0),
        )
    ]
    grad_specs = [
        pl.BlockSpec((3, STEP_ROWS, CHUNK), lambda i: (0, jnp.minimum(i, half_steps - 1), 0)),
        pl.BlockSpec((3, STEP_ROWS, CHUNK), lambda i: (0, jnp.maximum(i - half_steps, 0), 0)),
    ]
    return pl.pallas_call(
        expert_kernel,
        grid=(HIDDEN // STEP_ROWS,),
        in_specs=[SMEM]
        + [whole((ROWS, WIDTH))] * 4
        + [whole((rows, EXPERTS)), whole(wide.shape)]
        + weight_specs,
        out_specs=[
            whole((rows, EXPERTS)),
            whole((ROWS, WIDTH + 128)),
            whole((ROWS, WIDTH + 128)),
            whole((ROWS, WIDTH)),
            whole((ROWS, WIDTH)),
        ]
        + grad_specs * 4,
        out_shape=[
            jax.ShapeDtypeStruct((rows, EXPERTS), WIDE),
            jax.ShapeDtypeStruct((ROWS, WIDTH + 128), LOW),
            jax.ShapeDtypeStruct((ROWS, WIDTH + 128), LOW),
            jax.ShapeDtypeStruct((ROWS, WIDTH), LOW),
            jax.ShapeDtypeStruct((ROWS, WIDTH), LOW),
        ]
        + [jax.ShapeDtypeStruct((3, HIDDEN // 2, CHUNK), LOW)] * 8,
        scratch_shapes=[
            pltpu.VMEM((rows, WIDTH), LOW),
            pltpu.VMEM((rows, WIDTH), LOW),
            pltpu.VMEM((rows, WIDTH), WIDE),
            pltpu.VMEM((rows, WIDTH), WIDE),
            pltpu.VMEM((rows, EXPERTS), WIDE),
            pltpu.VMEM((rows, 2 * EXPERTS), LOW),
        ],
        compiler_params=pltpu.CompilerParams(
            vmem_limit_bytes=VMEM, dimension_semantics=("arbitrary",)
        ),
        cost_estimate=pl.CostEstimate(
            flops=25 * 10**9, bytes_accessed=3 * 10**7, transcendentals=0
        ),
        name="experts",
    )(
        core, x_own, x_far, dy_own, dy_far, named, wide,
        *[pieces[k][half] for _ in range(3) for k in range(4) for half in range(2)],
    )


def body(
    inputs,
    cotangent,
    routes,
    seq_lengths,
    block_order,
    attn_gain,
    query_weight,
    key_weight,
    value_weight,
    output_weight,
    ffn_gain,
    router_weight,
    gate_weight,
    up_weight,
    down_weight,
):
    dp = lax.axis_index("dp")
    ctx = lax.axis_index("ctx")
    tp = lax.axis_index("tp")
    core = ctx % 2

    core_at = core.reshape(1).astype(jnp.int32)
    tp_at = tp.reshape(1).astype(jnp.int32)
    dp_at = dp.reshape(1).astype(jnp.int32)

    small = jnp.concatenate(
        [
            query_weight.T,
            key_weight.T,
            value_weight.T,
            output_weight.T,
            router_weight.T,
            attn_gain[None],
            ffn_gain[None],
            jnp.zeros((14, CHUNK), LOW),
        ],
        axis=0,
    )
    small_parts = [small] + [from_dp(small, k) for k in (1, 2, 3)]

    rows_low = turn(inputs, dp * CHUNK)
    grad_low = turn(cotangent, dp * CHUNK)
    named = jnp.sum(
        (routes[:, :, None] == jnp.arange(EXPERTS, dtype=jnp.int32)[None, None, :]).astype(WIDE),
        axis=1,
    ).astype(LOW)
    grad_far = swap_ctx(grad_low, 1)
    named_both = jnp.concatenate([named, swap_ctx(named, 1)], axis=0)

    order = block_order[0]
    offsets = jnp.arange(BLOCK, dtype=jnp.int32)
    mine = lax.dynamic_slice_in_dim(order, ctx * SLOTS, SLOTS)
    my_places = (mine[:, None] * BLOCK + offsets[None, :]).reshape(ROWS, 1)
    lengths = seq_lengths[0]
    ends = jnp.cumsum(lengths)
    passed = (my_places >= ends[None, :]).astype(jnp.int32)
    my_first = jnp.sum(passed * lengths[None, :], axis=1, keepdims=True)
    inner = (my_places - my_first).astype(WIDE)
    by_slot = order.reshape(N_CTX, SLOTS).T.reshape(-1)
    key_places = (by_slot[:, None] * BLOCK + offsets[None, :]).reshape(1, N_CTX * ROWS)
    half = HEAD_DIM // 2
    freqs = 10000.0 ** (-jnp.arange(half, dtype=WIDE) / half)
    angle = inner * freqs[None, :]
    cosine = jnp.cos(angle)
    sine = jnp.sin(angle)
    cos_six = jnp.concatenate([cosine] * 6, axis=1)
    sin_six = jnp.concatenate([-sine, sine] * 3, axis=1)

    own = cut_weights(core_at, (gate_weight, up_weight, down_weight), small_parts[1:])
    right = [from_dp(part, 1) for part in own]
    left = [from_dp(part, 3) for part in own]
    across = [from_dp(right[0], 1), from_dp(left[1], 3)]
    pieces = [own, right, across, left]

    wide, out_w, normed, query, kv = local_call(
        project_kernel,
        [
            ((PACK_ROWS, WIDTH), LOW),
            ((128, WIDTH), LOW),
            ((ROWS, WIDTH), LOW),
            ((ROWS, 128), LOW),
            ((ROWS, 128), LOW),
        ],
        rows_low, *small_parts, cos_six, sin_six,
        name="project",
    )
    kv_all = lax.all_gather(kv, "ctx", axis=0, tiled=True)
    attended, attn_part, *probs = attend(
        query, kv_all, my_first, my_places, key_places, out_w, after=(right[0], left[0])
    )

    attn_parts = lax.all_to_all(attn_part, "tp", 0, 0, tiled=True).reshape(N_TP, PART, WIDTH)
    resid, normed_sent = local_call(
        norm_kernel,
        [((PART, WIDTH), WIDE), ((ROWS, WIDTH), LOW)],
        attn_parts, rows_low, wide,
        scalars=(tp_at,), after=(right[1], left[1], *across), name="norm",
    )
    normed_two = lax.all_to_all(normed_sent, "tp", 0, 0, tiled=True)
    normed_far = swap_ctx(normed_two, 1)

    dense, dx_own, dx_far, y_own, y_far, *grads = experts(
        core_at, normed_two, normed_far, grad_low, grad_far, named_both, wide, pieces
    )
    chunks = [grads[2 * k : 2 * k + 2] for k in range(4)]

    by_left = to_dp(chunks[2][0], 1)
    by_right = to_dp(chunks[2][1], 3)
    straight = [to_dp(chunks[3][0], 3), to_dp(chunks[1][1], 1)]

    dx = (dx_own.astype(WIDE) + swap_ctx(dx_far, 1).astype(WIDE)).astype(LOW)
    dx_parts = lax.all_to_all(dx, "tp", 0, 0, tiled=True).reshape(N_TP, PART, WIDTH + 128)
    relay_right = sum_parts([chunks[1][0], by_left])
    relay_left = sum_parts([chunks[3][1], by_right])
    dresid, gain_two_part, sent = local_call(
        norm_back_kernel,
        [((PART, WIDTH), WIDE), ((1, WIDTH), WIDE), ((ROWS, WIDTH + 128), LOW)],
        dx_parts, resid, dense, grad_low, wide,
        scalars=(tp_at,), after=(relay_right, relay_left), name="norm_back",
    )
    relayed = [to_dp(relay_right, 1), to_dp(relay_left, 3)]
    first, second = ([chunks[0][h], straight[h], relayed[h]] for h in range(2))
    back = lax.all_to_all(sent, "tp", 0, 0, tiled=True)
    dlogits_low = back[:, WIDTH : WIDTH + EXPERTS]
    first_half = sum_parts(first)
    first_other = swap_ctx(first_half, 2)
    dq, dkv = attend_back(query, kv_all, back, out_w, probs, after=(first_half,))
    y = sum_parts([y_own, swap_ctx(y_far, 1)], after=(dq, first_other))
    y_parts = lax.all_to_all(y, "tp", 0, 0, tiled=True).reshape(N_TP, PART, WIDTH)
    second_half = sum_parts(second, after=(y,))
    second_other = swap_ctx(second_half, 2)
    dkv_parts = lax.all_to_all(dkv, "ctx", 0, 0, tiled=True).reshape(N_CTX, ROWS, 128)
    dnorm_one, *small_chunks = local_call(
        project_back_kernel,
        [((ROWS, WIDTH + 128), LOW)] + [((GAIN_ROW, CHUNK), LOW)] * N_DP,
        dq, dkv_parts, cos_six, sin_six, normed, rows_low, wide,
        dot_tn(attended, back[:, :WIDTH]).astype(LOW),
        dot_tn(dlogits_low, normed_two).astype(LOW),
        gain_two_part,
        after=(second_half,),
        name="project_back", us=4.0,
    )

    dnorm_parts = lax.all_to_all(dnorm_one, "tp", 0, 0, tiled=True).reshape(
        N_TP, PART, WIDTH + 128
    )
    small_parts = [small_chunks[0]] + [to_dp(small_chunks[k], k) for k in (1, 2, 3)]
    sent, *gain_chunks = local_call(
        last_kernel,
        [((ROWS, 2 * WIDTH), LOW)] + [((16, CHUNK), LOW)] * N_DP,
        dnorm_parts, dresid, rows_low, wide, y_parts, resid,
        scalars=(jnp.concatenate([tp_at, dp_at]),), after=tuple(small_parts[1:]),
        name="last",
    )
    last = lax.all_to_all(sent, "tp", 0, 0, tiled=True)
    gain_parts = [gain_chunks[0]] + [to_dp(gain_chunks[k], k) for k in (1, 2, 3)]
    (small_sum,) = local_call(
        small_kernel, [((PACK_ROWS, CHUNK), LOW)], *small_parts, *gain_parts,
        after=(second_other,), name="small"
    )
    small_sum = sum_parts([small_sum, swap_ctx(small_sum, 1)])
    small_sum = small_sum.astype(WIDE) + swap_ctx(small_sum, 2).astype(WIDE)

    first_half = sum_parts([first_half, first_other], after=(sent,))
    second_half = sum_parts([second_half, second_other], after=(last,))
    block_output, input_grad, *expert_grads = place_grads(
        core_at,
        [first_half, swap_ctx(first_half, 1), second_half, swap_ctx(second_half, 1)],
        last,
    )
    return (
        block_output,
        input_grad,
        small_sum[GAIN_ROW],
        small_sum[:128].T,
        small_sum[128:192].T,
        small_sum[192:256].T,
        small_sum[256:384].T,
        small_sum[GAIN_ROW + 1],
        small_sum[384:416].T,
        *expert_grads,
    )


def solution(mesh):
    placed = (
        P(("dp", "ctx"), None),
        P(("dp", "ctx"), None),
        P(("dp", "ctx"), None),
        P("dp", None),
        P("dp", None),
        P("dp"),
        P("dp", "tp"),
        P("dp", "tp"),
        P("dp", "tp"),
        P("dp", "tp"),
        P("dp"),
        P("dp", None),
        P(None, "tp", "dp"),
        P(None, "tp", "dp"),
        P(None, "tp", "dp"),
    )
    return jax.shard_map(
        body,
        mesh=mesh,
        in_specs=placed,
        out_specs=(
            P(("dp", "ctx"), None),
            P(("dp", "ctx"), None),
            P("dp"),
            P("dp", "tp"),
            P("dp", "tp"),
            P("dp", "tp"),
            P("dp", "tp"),
            P("dp"),
            P("dp", None),
            P(None, "tp", "dp"),
            P(None, "tp", "dp"),
            P(None, "tp", "dp"),
        ),
        check_vma=False,
    )
```
